32 devices in a mesh: pack: 8 (over z, x), seq: 4 (over y, core).
Axes of the slice: x: 2, y: 2, z: 4, core: 2. Of those that a mesh axis runs over, the one named last changes fastest.
Arguments:
- source: bfloat16 [4, 1536, 1152], P('seq', 'pack')
- destination: int32 [4, 1536], P('seq', 'pack'), may hold values from 0 to 1535, as said below
- doc_ids: int32 [8, 768], P('pack'), may hold values from 0 to 5, as said below
- w_qkv: bfloat16 [3, 1152, 1152], P(None, None, 'seq')
- w_out: bfloat16 [1152, 1152], P('seq'), may hold values from -0.1875 to 0.1875
Outputs:
- projected: bfloat16 [8, 768, 1152], P('pack', 'seq')
The draws below stay inside these ranges and needn't reach their ends.
Inputs may be any that keep to these rules, and one draw needn't show every extreme that they name: For every column s, destination[s] is a permutation of 0 to 1535. Of the 192 rows of one device, at most 48 have the same destination // 192, and in every column some device sends exactly 48 rows to one owner. doc_ids[p] starts at 0, never falls, rises by one at most from one position to the next and changes only at positions that are multiples of 128; some packed row reaches the largest value.
All inputs are finite; a program needn't handle non-finite values.
Results may differ from the reference program's by a relative error of at most 0.011.
Values may be sent and summed in bfloat16 or wider, within the bound.
A program may use at most 64 MiB of HBM per device.

```python
import math
import jax
import jax.numpy as jnp
from jax import lax

D = 1152
H = 16
HD = 72
TOK_DEV = 192
DOC_BLOCK = 128
ROW_LEN = 768
N_PACK = 8
N_SEQ = 4


def draw_destination(key, part):
    key = jax.random.fold_in(key, 11)
    first, second, third = jax.random.split(key, 3)
    base = TOK_DEV // N_PACK
    excess = jax.random.randint(first, (N_SEQ, N_PACK), 0, base + 1)
    excess = excess.at[:, 0].set(base).at[:, 1].set(0)
    counts = base + excess - jnp.roll(excess, -1, axis=1)
    ends = jnp.cumsum(counts, axis=1)
    keys_one = jax.random.split(second, N_SEQ * N_PACK)
    ranks = jax.vmap(lambda single: jax.random.permutation(single, TOK_DEV))(keys_one).reshape(N_SEQ, N_PACK, TOK_DEV)
    keys_two = jax.random.split(third, N_SEQ * N_PACK)
    arrival = jax.vmap(lambda single: jax.random.permutation(single, TOK_DEV))(keys_two).reshape(N_SEQ, N_PACK * TOK_DEV)
    offset = jnp.sum(ranks[..., None] >= ends[:, None, None, :], axis=-1).astype(jnp.int32)
    sender = jnp.arange(N_PACK, dtype=jnp.int32)[None, :, None]
    owner = (sender + offset) % N_PACK
    lookup = (owner * TOK_DEV + ranks).reshape(N_SEQ, N_PACK * TOK_DEV)
    places = jnp.take_along_axis(arrival, lookup, axis=1)
    return (owner.reshape(N_SEQ, N_PACK * TOK_DEV) * TOK_DEV + places).astype(jnp.int32)


def draw_doc_ids(key, part):
    key = jax.random.fold_in(key, 13)
    blocks = ROW_LEN // DOC_BLOCK
    starts = (jax.random.randint(key, (N_PACK, blocks), 0, 4) == 0).astype(jnp.int32)
    starts = starts.at[0, :].set(1)
    starts = starts.at[:, 0].set(0)
    numbers = jnp.cumsum(starts, axis=1)
    return jnp.repeat(numbers, DOC_BLOCK, axis=1).astype(jnp.int32)


def draw_source(key, part):
    key = jax.random.fold_in(key, 5)
    first = jax.random.fold_in(key, 0)
    shape = (N_SEQ, N_PACK * TOK_DEV, D)
    values = jax.random.normal(first, shape, jnp.float32)
    return values.astype(jnp.bfloat16)


def draw_w_qkv(key, part):
    key = jax.random.fold_in(key, 7)
    first, second, third = jax.random.split(key, 3)
    shape = (D, D)
    query_w = jax.random.normal(first, shape, jnp.float32)
    key_w = jax.random.normal(second, shape, jnp.float32)
    value_w = jax.random.normal(third, shape, jnp.float32)
    return (jnp.stack([query_w, key_w, value_w]) * D ** (-0.5)).astype(jnp.bfloat16)


def levels(key, dims, cuts, low, largest):
    gain = 1.0
    for axis_at, parts in cuts:
        steps = jax.random.uniform(jax.random.fold_in(jax.random.fold_in(key, 6), axis_at), (parts,), jnp.float32, low / len(cuts), largest / len(cuts))
        gain = gain * jnp.repeat(jnp.exp(steps), dims[axis_at] // parts).reshape((-1,) + (1,) * (len(dims) - 1 - axis_at))
    return gain


def centred(own_key, shape, deviation, reach, cuts=(), kind=jnp.bfloat16):
    gain = levels(own_key, shape, cuts, -0.22, 0.18) if cuts else 1.0
    result = jax.random.normal(own_key, shape, jnp.float32) * deviation * gain
    return jnp.minimum(jnp.maximum(result, -reach), reach).astype(kind)


def setup_inputs(seed: int = 0) -> dict:
    keys = jax.random.split(jax.random.key(seed), 6)
    return {
        "source": draw_source(jax.random.fold_in(keys[5], 71), 0),
        "destination": draw_destination(jax.random.fold_in(keys[5], 71), 0),
        "doc_ids": draw_doc_ids(jax.random.fold_in(keys[5], 71), 0),
        "w_qkv": draw_w_qkv(jax.random.fold_in(keys[5], 71), 0),
        "w_out": centred(keys[4], (D, D), D ** -0.5, 0.1875, ((0, 4),)),
    }


def attend_head(queries, key_rows, value_rows, same_doc):
    scores = jnp.dot(queries, key_rows.T, preferred_element_type=jnp.float32) / math.sqrt(HD)
    scores = jnp.where(same_doc, scores, -jnp.inf)
    highest = lax.optimization_barrier(jnp.max(scores, axis=1, keepdims=True))
    expo = jnp.exp(scores - highest)
    weights = (expo / lax.optimization_barrier(jnp.sum(expo, axis=1, keepdims=True))).astype(jnp.bfloat16)
    return jnp.dot(weights, value_rows, preferred_element_type=jnp.float32).astype(jnp.bfloat16)

def reference(source, destination, doc_ids, w_qkv, w_out):
    column = jnp.arange(N_SEQ, dtype=jnp.int32)[:, None]
    target = destination // TOK_DEV * ROW_LEN + column * TOK_DEV + destination % TOK_DEV
    packed = jnp.zeros((N_PACK * ROW_LEN, D), jnp.bfloat16)
    packed = packed.at[target.reshape(-1)].set(source.reshape(-1, D)).reshape(N_PACK, ROW_LEN, D)

    def one_row(inputs):
        tokens, documents = inputs
        stacked = jnp.stack([jnp.dot(tokens, w_qkv[which], preferred_element_type=jnp.float32) for which in range(3)]).astype(jnp.bfloat16)
        by_head = stacked.reshape(3, ROW_LEN, H, HD).transpose(2, 0, 1, 3)
        same_doc = documents[:, None] == documents[None, :]
        heads_out = lax.map(lambda grouped: attend_head(grouped[0], grouped[1], grouped[2], same_doc), by_head)
        merged = heads_out.transpose(1, 0, 2).reshape(ROW_LEN, D)
        return jnp.dot(merged, w_out, preferred_element_type=jnp.float32).astype(jnp.bfloat16)
    return lax.map(one_row, (packed, doc_ids))
```

```python
import functools
import math

import jax
import jax.numpy as jnp
from jax import lax
from jax.experimental import pallas as pl
from jax.experimental.pallas import tpu as pltpu
from jax.sharding import PartitionSpec as P

HD = 72
CORES = 2
MESH = pl.DeviceIdType.MESH
F32 = jnp.float32
BF16 = jnp.bfloat16


def head_window(head, group):
    lower = head * HD // 128 * 128
    upper = min(-(-(head + 1) * HD // 128) * 128, group)
    return lower, upper


def kernel(
    n, rows_y, cap, pieces,
    src, dst, doc, wqkv, wout, out,
    outbox, inbox, lab_out, lab_in, packed, acc, qkv, doc_col, att_acc, att_out, att_in, w_all,
    disp_send, disp_recv, lab_send, lab_recv,
    tok_send, tok_recv, tokf_send, tokf_recv,
    w_send, w_recv, wf_send, wf_recv, att_send, att_recv,
):
    n_seq = rows_y * CORES
    tok = src.shape[1]
    wide = src.shape[2] // pieces
    group = wout.shape[0]
    length = doc.shape[1]
    heads = group // HD
    me = lax.axis_index("pack")
    seq = lax.axis_index("seq")
    my_y, my_c = seq // CORES, seq % CORES
    sib = (me, my_y * CORES + 1 - my_c)

    def on_y(d):
        return (me, (my_y + d) % rows_y * CORES + my_c)

    def remote(source, target, ss, rs, device):
        return pltpu.make_async_remote_copy(
            src_ref=source, dst_ref=target, send_sem=ss, recv_sem=rs,
            device_id=device, device_id_type=MESH,
        )

    barrier = pltpu.get_barrier_semaphore()
    for k in range(1, n):
        pl.semaphore_signal(barrier, inc=1, device_id=((me + k) % n, seq), device_id_type=MESH)
    for k in range(1, n_seq):
        pl.semaphore_signal(barrier, inc=1, device_id=(me, (seq + k) % n_seq), device_id_type=MESH)

    dest = dst[...]
    steps = lax.broadcasted_iota(jnp.int32, (n, tok), 0)
    owners = jnp.sum((dest >= (steps + 1) * tok).astype(jnp.int32), axis=0, keepdims=True)
    places = dest - owners * tok
    shift = owners - me
    shift = jnp.where(shift < 0, shift + n, shift)
    matches = (steps == shift).astype(F32)
    before = lax.broadcasted_iota(jnp.int32, (tok, tok), 0) <= lax.broadcasted_iota(jnp.int32, (tok, tok), 1)
    counted = jnp.dot(matches.astype(BF16), before.astype(F32).astype(BF16), preferred_element_type=F32)
    slots = jnp.sum(matches * counted, axis=0, keepdims=True).astype(jnp.int32) - 1
    flat = shift * cap + slots
    chosen = (lax.broadcasted_iota(jnp.int32, (n * cap, tok), 0) == flat).astype(F32).astype(BF16)
    named = jnp.broadcast_to((places + 1).astype(F32), (8, tok)).astype(BF16)
    lab_out[...] = lax.dot_general(named, chosen, (((1,), (1,)), ((), ())), preferred_element_type=F32)

    def column(c):
        return pl.ds(c * wide, wide)

    def fill(c):
        outbox[c] = jnp.dot(chosen, src[0, :, column(c)], preferred_element_type=F32).astype(BF16)
        inbox[c, 0:cap] = outbox[c, 0:cap]

    def label_copy(k):
        return remote(lab_out, lab_in.at[k], lab_send.at[k], lab_recv.at[k], ((me + k) % n, seq))

    def dispatch_copy(c, k):
        block = pl.ds(k * cap, cap)
        return remote(
            outbox.at[c, block], inbox.at[c, block], disp_send.at[c, k], disp_recv.at[c, k],
            ((me + k) % n, seq),
        )

    def token_copy(c, d, at_y):
        place = packed.at[c, at_y, my_c]
        return remote(place, place, tok_send.at[c, d], tok_recv.at[c, d], on_y(d) if d else sib)

    def token_forward(c, d, at_c):
        place = packed.at[c, (my_y - d) % rows_y, at_c]
        return remote(place, place, tokf_send.at[c, d], tokf_recv.at[c, d], sib)

    def weight_copy(c, d):
        return remote(
            wout.at[:, column(c)], w_all.at[c, my_y, my_c], w_send.at[c, d], w_recv.at[c, d],
            on_y(d) if d else sib,
        )

    def weight_forward(c, d, at_c):
        place = w_all.at[c, (my_y - d) % rows_y, at_c]
        return remote(place, place, wf_send.at[c, d], wf_recv.at[c, d], sib)

    fill(0)
    pl.semaphore_wait(barrier, n - 1 + n_seq - 1)
    for k in range(1, n):
        label_copy(k).start()
    for c in range(pieces):
        if c:
            fill(c)
        for k in range(1, n):
            dispatch_copy(c, k).start()

    def send_weights(c):
        for d in range(1, rows_y):
            weight_copy(c, d).start()
        weight_copy(c, 0).start()

    def forward_weights(c):
        for d in range(1, rows_y):
            weight_copy(c, d).wait_recv()
            weight_forward(c, d, my_c).start()

    send_weights(0)

    doc_row = doc[...].astype(F32)
    doc_col[...] = jnp.broadcast_to(doc_row, (128, length)).T.reshape(doc_col.shape)

    lane = lax.broadcasted_iota(jnp.int32, (1, n * cap), 1)
    label = jnp.where(lane < cap, lab_out[0:1, :], 0.0)
    for k in range(1, n):
        label_copy(k).wait_recv()
        label = jnp.where((lane >= k * cap) & (lane < (k + 1) * cap), lab_in[k, 0:1, :], label)
    rows = lax.broadcasted_iota(jnp.int32, (tok, n * cap), 0) + 1
    placing = (rows.astype(F32) == label).astype(F32).astype(BF16)

    def project(c, at_y):
        block = packed[c, at_y].reshape(CORES * tok, wide)
        for j in range(3):
            part = jnp.dot(block, wqkv[j, column(c), :], preferred_element_type=F32)
            if c:
                part = part + acc[j, at_y]
            if c < pieces - 1:
                acc[j, at_y] = part
            else:
                qkv[j, at_y] = part.astype(BF16).reshape(CORES, tok, group)

    def consume(c):
        for d in range(1, rows_y):
            token_copy(c, d, (my_y - d) % rows_y).wait_recv()
            token_forward(c, d, my_c).start()
        token_copy(c, 0, my_y).wait_recv()
        project(c, my_y)
        for d in range(1, rows_y):
            token_forward(c, d, 1 - my_c).wait_recv()
            project(c, (my_y - d) % rows_y)

    for c in range(pieces):
        for k in range(1, n):
            dispatch_copy(c, k).wait_recv()
        packed[c, my_y, my_c] = jnp.dot(placing, inbox[c], preferred_element_type=F32).astype(BF16)
        for d in range(1, rows_y):
            token_copy(c, d, my_y).start()
        token_copy(c, 0, my_y).start()
        if c:
            send_weights(c)
            consume(c - 1)
            forward_weights(c - 1)
    consume(pieces - 1)

    factor = math.log2(math.e) / math.sqrt(HD)

    def target(i):
        at_y = (my_y + i // CORES + 1) % rows_y
        at_c = (my_c + 1 - i % CORES) % CORES
        return at_y, at_c

    def attended_copy(i):
        at_y, at_c = target(i)
        return remote(
            att_out.at[i], att_in.at[i], att_send.at[i], att_recv.at[i], (me, at_y * CORES + at_c)
        )

    def attend(i, carry):
        at_y, at_c = target(i)
        same = doc_col[at_y, at_c][:, 0:1] == doc_row
        att_acc[...] = jnp.zeros_like(att_acc)
        for h in range(heads):
            lower, upper = head_window(h, group)
            lanes = lax.broadcasted_iota(jnp.int32, (1, upper - lower), 1) + lower
            mine = (lanes >= h * HD) & (lanes < (h + 1) * HD)
            query = jnp.where(mine, qkv[0, at_y, at_c, :, lower:upper].astype(F32), 0.0).astype(BF16)
            keys = qkv[1, :, :, :, lower:upper].reshape(length, upper - lower)
            values = qkv[2, :, :, :, lower:upper].reshape(length, upper - lower)
            scores = lax.dot_general(query, keys, (((1,), (1,)), ((), ())), preferred_element_type=F32)
            scores = jnp.where(same, scores, -jnp.inf)
            expo = jnp.exp2((scores - jnp.max(scores, axis=1, keepdims=True)) * factor)
            total = jnp.sum(expo, axis=1, keepdims=True)
            mixed = jnp.dot(expo.astype(BF16), values, preferred_element_type=F32) / total
            att_acc[:, lower:upper] += jnp.where(mine, mixed, 0.0)
        att_out[i] = att_acc[...].astype(BF16)

        @pl.when(i < n_seq - 1)
        def _():
            attended_copy(i).start()

        return carry

    lax.fori_loop(0, n_seq, attend, 0)
    forward_weights(pieces - 1)

    own = att_out[n_seq - 1]
    totals = [jnp.dot(own, wout[:, column(c)], preferred_element_type=F32) for c in range(pieces)]
    for c in range(pieces):
        weight_copy(c, 0).wait_recv()
        for d in range(1, rows_y):
            weight_forward(c, d, 1 - my_c).wait_recv()
    for i in range(n_seq - 2, -1, -1):
        attended_copy(i).wait_recv()
        from_y = (my_y - (i // CORES + 1)) % rows_y
        from_c = (my_c - (1 - i % CORES)) % CORES
        arrived = att_in[i]
        totals = [
            totals[c] + jnp.dot(arrived, w_all[c, from_y, from_c], preferred_element_type=F32)
            for c in range(pieces)
        ]
    for c in range(pieces):
        out[0, :, column(c)] = totals[c].astype(BF16)

    for k in range(1, n):
        label_copy(k).wait_send()
    for c in range(pieces):
        for k in range(1, n):
            dispatch_copy(c, k).wait_send()
        for d in range(rows_y):
            token_copy(c, d, my_y).wait_send()
            weight_copy(c, d).wait_send()
            if d:
                token_forward(c, d, my_c).wait_send()
                weight_forward(c, d, my_c).wait_send()
    for i in range(n_seq - 1):
        attended_copy(i).wait_send()


def body(source, destination, doc_ids, w_qkv, w_out):
    n = lax.axis_size("pack")
    n_seq = lax.axis_size("seq")
    rows_y = n_seq // CORES
    tok, width = source.shape[1:]
    group = w_out.shape[0]
    length = doc_ids.shape[1]
    cap = -(-(2 * tok // n) // 16) * 16
    pieces = 3
    wide = width // pieces
    dma = pltpu.SemaphoreType.DMA
    vmem = pl.BlockSpec(memory_space=pltpu.VMEM)
    return pl.pallas_call(
        functools.partial(kernel, n, rows_y, cap, pieces),
        out_shape=jax.ShapeDtypeStruct((1, tok, width), BF16),
        in_specs=[vmem] * 5,
        out_specs=vmem,
        scratch_shapes=[
            pltpu.VMEM((pieces, n * cap, wide), BF16),
            pltpu.VMEM((pieces, n * cap, wide), BF16),
            pltpu.VMEM((8, n * cap), F32),
            pltpu.VMEM((n, 8, n * cap), F32),
            pltpu.VMEM((pieces, rows_y, CORES, tok, wide), BF16),
            pltpu.VMEM((3, rows_y, CORES * tok, group), F32),
            pltpu.VMEM((3, rows_y, CORES, tok, group), BF16),
            pltpu.VMEM((rows_y, CORES, tok, 128), F32),
            pltpu.VMEM((tok, group), F32),
            pltpu.VMEM((n_seq, tok, group), BF16),
            pltpu.VMEM((n_seq, tok, group), BF16),
            pltpu.VMEM((pieces, rows_y, CORES, group, wide), BF16),
            dma((pieces, n)), dma((pieces, n)), dma((n,)), dma((n,)),
            dma((pieces, rows_y)), dma((pieces, rows_y)), dma((pieces, rows_y)), dma((pieces, rows_y)),
            dma((pieces, rows_y)), dma((pieces, rows_y)), dma((pieces, rows_y)), dma((pieces, rows_y)),
            dma((n_seq,)), dma((n_seq,)),
        ],
        compiler_params=pltpu.CompilerParams(
            collective_id=0, has_side_effects=True, vmem_limit_bytes=56 * 1024 * 1024
        ),
        cost_estimate=pl.CostEstimate(flops=4_000_000_000, bytes_accessed=4_000_000, transcendentals=2_400_000),
    )(source, destination, doc_ids, w_qkv, w_out)


def solution(mesh):
    placed = (
        P("seq", "pack", None),
        P("seq", "pack"),
        P("pack", None),
        P(None, None, "seq"),
        P("seq", None),
    )
    return jax.shard_map(
        body, mesh=mesh, in_specs=placed, out_specs=P("pack", "seq", None), check_vma=False
    )
```

```python
import functools
import math

import jax
import jax.numpy as jnp
from jax import lax
from jax.experimental import pallas as pl
from jax.experimental.pallas import tpu as pltpu
from jax.sharding import PartitionSpec as P

HD = 72
CORES = 2
MESH = pl.DeviceIdType.MESH
F32 = jnp.float32
BF16 = jnp.bfloat16


def head_window(head, group):
    lower = head * HD // 128 * 128
    upper = min(-(-(head + 1) * HD // 128) * 128, group)
    return lower, upper


def kernel(
    n, rows_y, cap, pieces,
    src, dst, doc, wqkv_hbm, wout_hbm, out,
    wqkv, outbox, inbox, lab_out, lab_in, packed, acc, qkv, doc_col, att_acc, att_out, att_in, w_all,
    disp_send, disp_recv, lab_send, lab_recv,
    tok_send, tok_recv, tokf_send, tokf_recv,
    w_send, w_recv, wf_send, wf_recv, att_send, att_recv, load_sem,
):
    n_seq = rows_y * CORES
    tok = src.shape[1]
    group = wout_hbm.shape[0]
    length = doc.shape[1]
    heads = group // HD
    me = lax.axis_index("pack")
    seq = lax.axis_index("seq")
    my_y, my_c = seq // CORES, seq % CORES
    sib = (me, my_y * CORES + 1 - my_c)

    def on_y(d):
        return (me, (my_y + d) % rows_y * CORES + my_c)

    def remote(source, target, ss, rs, device):
        return pltpu.make_async_remote_copy(
            src_ref=source, dst_ref=target, send_sem=ss, recv_sem=rs,
            device_id=device, device_id_type=MESH,
        )

    load_qkv = pltpu.make_async_copy(wqkv_hbm, wqkv, load_sem.at[0])
    load_out = pltpu.make_async_copy(wout_hbm, w_all.at[my_y, my_c], load_sem.at[1])
    load_out.start()
    load_qkv.start()

    barrier = pltpu.get_barrier_semaphore()
    for k in range(1, n):
        pl.semaphore_signal(barrier, inc=1, device_id=((me + k) % n, seq), device_id_type=MESH)
    for k in range(1, n_seq):
        pl.semaphore_signal(barrier, inc=1, device_id=(me, (seq + k) % n_seq), device_id_type=MESH)

    dest = dst[...]
    steps = lax.broadcasted_iota(jnp.int32, (n, tok), 0)
    owners = jnp.sum((dest >= (steps + 1) * tok).astype(jnp.int32), axis=0, keepdims=True)
    places = dest - owners * tok
    shift = owners - me
    shift = jnp.where(shift < 0, shift + n, shift)
    matches = (steps == shift).astype(F32)
    before = lax.broadcasted_iota(jnp.int32, (tok, tok), 0) <= lax.broadcasted_iota(jnp.int32, (tok, tok), 1)
    counted = jnp.dot(matches.astype(BF16), before.astype(F32).astype(BF16), preferred_element_type=F32)
    slots = jnp.sum(matches * counted, axis=0, keepdims=True).astype(jnp.int32) - 1
    flat = shift * cap + slots
    chosen = (lax.broadcasted_iota(jnp.int32, (n * cap, tok), 0) == flat).astype(F32).astype(BF16)
    named = jnp.broadcast_to((places + 1).astype(F32), (8, tok)).astype(BF16)
    lab_out[...] = lax.dot_general(named, chosen, (((1,), (1,)), ((), ())), preferred_element_type=F32)

    def column(c):
        return pl.ds(*pieces[c])

    def fill(c):
        moved = jnp.dot(chosen, src[0, :, column(c)], preferred_element_type=F32).astype(BF16)
        outbox[:, column(c)] = moved
        inbox[0:cap, column(c)] = moved[0:cap]

    def label_copy(k):
        return remote(lab_out, lab_in.at[k], lab_send.at[k], lab_recv.at[k], ((me + k) % n, seq))

    def dispatch_copy(c, k):
        block = pl.ds(k * cap, cap)
        return remote(
            outbox.at[block, column(c)], inbox.at[block, column(c)], disp_send.at[c, k], disp_recv.at[c, k],
            ((me + k) % n, seq),
        )

    def token_copy(c, d, at_y):
        place = packed.at[at_y, my_c, :, column(c)]
        return remote(place, place, tok_send.at[c, d], tok_recv.at[c, d], on_y(d) if d else sib)

    def token_forward(c, d, at_c):
        place = packed.at[(my_y - d) % rows_y, at_c, :, column(c)]
        return remote(place, place, tokf_send.at[c, d], tokf_recv.at[c, d], sib)

    def weight_copy(c, d):
        place = w_all.at[my_y, my_c, :, column(c)]
        return remote(place, place, w_send.at[c, d], w_recv.at[c, d], on_y(d) if d else sib)

    def weight_forward(c, d, at_c):
        place = w_all.at[(my_y - d) % rows_y, at_c, :, column(c)]
        return remote(place, place, wf_send.at[c, d], wf_recv.at[c, d], sib)

    fill(0)
    pl.semaphore_wait(barrier, n - 1 + n_seq - 1)
    for k in range(1, n):
        label_copy(k).start()
    for c in range(len(pieces)):
        if c:
            fill(c)
        for k in range(1, n):
            dispatch_copy(c, k).start()

    def send_weights(c):
        for d in range(1, rows_y):
            weight_copy(c, d).start()
        weight_copy(c, 0).start()

    def forward_weights(c):
        for d in range(1, rows_y):
            weight_copy(c, d).wait_recv()
            weight_forward(c, d, my_c).start()

    load_out.wait()
    send_weights(0)

    doc_row = doc[...].astype(F32)
    doc_col[...] = jnp.broadcast_to(doc_row, (128, length)).T.reshape(doc_col.shape)

    lane = lax.broadcasted_iota(jnp.int32, (1, n * cap), 1)
    label = jnp.where(lane < cap, lab_out[0:1, :], 0.0)
    for k in range(1, n):
        label_copy(k).wait_recv()
        label = jnp.where((lane >= k * cap) & (lane < (k + 1) * cap), lab_in[k, 0:1, :], label)
    rows = lax.broadcasted_iota(jnp.int32, (tok, n * cap), 0) + 1
    placing = (rows.astype(F32) == label).astype(F32).astype(BF16)

    def project(c, at_y):
        block = packed[at_y, :, :, column(c)].reshape(CORES * tok, pieces[c][1])
        for j in range(3):
            part = lax.dot_general(
                block, wqkv[j, :, column(c)], (((1,), (1,)), ((), ())), preferred_element_type=F32
            )
            if c:
                part = part + acc[j, at_y]
            if c < len(pieces) - 1:
                acc[j, at_y] = part
            else:
                qkv[j, at_y] = part.astype(BF16).reshape(CORES, tok, group)

    def consume(c):
        for d in range(1, rows_y):
            token_copy(c, d, (my_y - d) % rows_y).wait_recv()
            token_forward(c, d, my_c).start()
        token_copy(c, 0, my_y).wait_recv()
        project(c, my_y)
        for d in range(1, rows_y):
            token_forward(c, d, 1 - my_c).wait_recv()
            project(c, (my_y - d) % rows_y)

    load_qkv.wait()
    for c in range(len(pieces)):
        for k in range(1, n):
            dispatch_copy(c, k).wait_recv()
        packed[my_y, my_c, :, column(c)] = jnp.dot(
            placing, inbox[:, column(c)], preferred_element_type=F32
        ).astype(BF16)
        for d in range(1, rows_y):
            token_copy(c, d, my_y).start()
        token_copy(c, 0, my_y).start()
        if c:
            send_weights(c)
            consume(c - 1)
            forward_weights(c - 1)
    consume(len(pieces) - 1)

    factor = math.log2(math.e) / math.sqrt(HD)

    def attended_copy(i, at_c, to):
        return remote(
            att_out.at[i, at_c], att_in.at[i, my_c], att_send.at[i, at_c], att_recv.at[i, my_c], to
        )

    def arrival(i, at_c):
        place = att_in.at[i, at_c]
        return remote(place, place, att_send.at[i, at_c], att_recv.at[i, at_c], sib)

    def attend(i, carry):
        at_y = (my_y + i + 1) % rows_y
        same = doc_col[at_y][:, 0:1] == doc_row
        att_acc[...] = jnp.zeros_like(att_acc)
        for h in range(heads):
            lower, upper = head_window(h, group)
            lanes = lax.broadcasted_iota(jnp.int32, (1, upper - lower), 1) + lower
            mine = (lanes >= h * HD) & (lanes < (h + 1) * HD)
            query = qkv[0, at_y, :, :, lower:upper].reshape(CORES * tok, upper - lower)
            query = jnp.where(mine, query.astype(F32), 0.0).astype(BF16)
            keys = qkv[1, :, :, :, lower:upper].reshape(length, upper - lower)
            values = qkv[2, :, :, :, lower:upper].reshape(length, upper - lower)
            scores = lax.dot_general(query, keys, (((1,), (1,)), ((), ())), preferred_element_type=F32)
            scores = jnp.where(same, scores, -jnp.inf)
            expo = jnp.exp2((scores - jnp.max(scores, axis=1, keepdims=True)) * factor)
            total = jnp.sum(expo, axis=1, keepdims=True)
            mixed = jnp.dot(expo.astype(BF16), values, preferred_element_type=F32) / total
            att_acc[:, lower:upper] += jnp.where(mine, mixed, 0.0)
        att_out[i] = att_acc[...].astype(BF16).reshape(CORES, tok, group)

        @pl.when(i < rows_y - 1)
        def _():
            for at_c in range(CORES):
                attended_copy(i, at_c, (me, at_y * CORES + at_c)).start()

        return carry

    lax.fori_loop(0, rows_y, attend, 0)
    last = rows_y - 1
    attended_copy(last, 1 - my_c, sib).start()
    forward_weights(len(pieces) - 1)

    def mixed_out(rows, at_y, at_c):
        return jnp.dot(rows, w_all[at_y, at_c], preferred_element_type=F32)

    total = mixed_out(att_out[last, my_c], my_y, my_c)
    for c in range(len(pieces)):
        weight_copy(c, 0).wait_recv()
        for d in range(1, rows_y):
            weight_forward(c, d, 1 - my_c).wait_recv()
    for i in range(rows_y - 1):
        for at_c in range(CORES):
            arrival(i, at_c).wait_recv()
            total = total + mixed_out(att_in[i, at_c], (my_y - i - 1) % rows_y, at_c)
    arrival(last, 1 - my_c).wait_recv()
    total = total + mixed_out(att_in[last, 1 - my_c], my_y, 1 - my_c)
    out[0] = total.astype(BF16)

    for k in range(1, n):
        label_copy(k).wait_send()
    for c in range(len(pieces)):
        for k in range(1, n):
            dispatch_copy(c, k).wait_send()
        for d in range(rows_y):
            token_copy(c, d, my_y).wait_send()
            weight_copy(c, d).wait_send()
            if d:
                token_forward(c, d, my_c).wait_send()
                weight_forward(c, d, my_c).wait_send()
    for i in range(rows_y - 1):
        for at_c in range(CORES):
            attended_copy(i, at_c, sib).wait_send()
    attended_copy(last, 1 - my_c, sib).wait_send()


def body(source, destination, doc_ids, w_qkv, w_out):
    n = lax.axis_size("pack")
    n_seq = lax.axis_size("seq")
    rows_y = n_seq // CORES
    tok, width = source.shape[1:]
    group = w_out.shape[0]
    length = doc_ids.shape[1]
    cap = -(-(2 * tok // n) // 16) * 16
    tiles = width // 128
    ends = [0, tiles - tiles * 5 // 9, tiles - tiles * 2 // 9, tiles]
    pieces = [(start * 128, (end - start) * 128) for start, end in zip(ends, ends[1:])]
    parts = len(pieces)
    dma = pltpu.SemaphoreType.DMA
    vmem = pl.BlockSpec(memory_space=pltpu.VMEM)
    return pl.pallas_call(
        functools.partial(kernel, n, rows_y, cap, pieces),
        out_shape=jax.ShapeDtypeStruct((1, tok, width), BF16),
        in_specs=[vmem] * 3 + [pl.BlockSpec(memory_space=pl.ANY)] * 2,
        out_specs=vmem,
        scratch_shapes=[
            pltpu.VMEM((3, group, width), BF16),
            pltpu.VMEM((n * cap, width), BF16),
            pltpu.VMEM((n * cap, width), BF16),
            pltpu.VMEM((8, n * cap), F32),
            pltpu.VMEM((n, 8, n * cap), F32),
            pltpu.VMEM((rows_y, CORES, tok, width), BF16),
            pltpu.VMEM((3, rows_y, CORES * tok, group), F32),
            pltpu.VMEM((3, rows_y, CORES, tok, group), BF16),
            pltpu.VMEM((rows_y, CORES * tok, 128), F32),
            pltpu.VMEM((CORES * tok, group), F32),
            pltpu.VMEM((rows_y, CORES, tok, group), BF16),
            pltpu.VMEM((rows_y, CORES, tok, group), BF16),
            pltpu.VMEM((rows_y, CORES, group, width), BF16),
            dma((parts, n)), dma((parts, n)), dma((n,)), dma((n,)),
            dma((parts, rows_y)), dma((parts, rows_y)), dma((parts, rows_y)), dma((parts, rows_y)),
            dma((parts, rows_y)), dma((parts, rows_y)), dma((parts, rows_y)), dma((parts, rows_y)),
            dma((rows_y, CORES)), dma((rows_y, CORES)), dma((2,)),
        ],
        compiler_params=pltpu.CompilerParams(
            collective_id=0, has_side_effects=True, vmem_limit_bytes=56 * 1024 * 1024
        ),
        cost_estimate=pl.CostEstimate(flops=4_000_000_000, bytes_accessed=4_000_000, transcendentals=2_400_000),
    )(source, destination, doc_ids, jnp.swapaxes(w_qkv, 1, 2), w_out)


def solution(mesh):
    placed = (
        P("seq", "pack", None),
        P("seq", "pack"),
        P("pack", None),
        P(None, None, "seq"),
        P("seq", None),
    )
    return jax.shard_map(
        body, mesh=mesh, in_specs=placed, out_specs=P("pack", "seq", None), check_vma=False
    )
```

```python
import functools
import math

import jax
import jax.numpy as jnp
from jax import lax
from jax.experimental import pallas as pl
from jax.experimental.pallas import tpu as pltpu
from jax.sharding import PartitionSpec as P

HD = 72
CORES = 2
MESH = pl.DeviceIdType.MESH
F32 = jnp.float32
BF16 = jnp.bfloat16


def head_window(head, group):
    lower = head * HD // 128 * 128
    upper = min(-(-(head + 1) * HD // 128) * 128, group)
    return lower, upper


def kernel(
    n, rows_y, cap, pieces,
    src, dst, doc, wqkv_hbm, wout_hbm, out,
    wqkv, outbox, inbox, lab_out, lab_in, packed, acc, qkv, doc_col, att_acc, att_out, att_in, w_all,
    disp_send, disp_recv, lab_send, lab_recv,
    tok_send, tok_recv, tokf_send, tokf_recv,
    w_send, w_recv, wf_send, wf_recv, att_send, att_recv, load_sem,
):
    n_seq = rows_y * CORES
    tok = src.shape[1]
    group = wout_hbm.shape[0]
    length = doc.shape[1]
    heads = group // HD
    me = lax.axis_index("pack")
    seq = lax.axis_index("seq")
    my_y, my_c = seq // CORES, seq % CORES
    sib = (me, my_y * CORES + 1 - my_c)

    def on_y(d):
        return (me, (my_y + d) % rows_y * CORES + my_c)

    def remote(source, target, ss, rs, device):
        return pltpu.make_async_remote_copy(
            src_ref=source, dst_ref=target, send_sem=ss, recv_sem=rs,
            device_id=device, device_id_type=MESH,
        )

    load_qkv = pltpu.make_async_copy(wqkv_hbm, wqkv, load_sem.at[0])
    load_out = pltpu.make_async_copy(wout_hbm, w_all.at[my_y, my_c], load_sem.at[1])
    load_out.start()
    load_qkv.start()

    barrier = pltpu.get_barrier_semaphore()
    for k in range(1, n):
        pl.semaphore_signal(barrier, inc=1, device_id=((me + k) % n, seq), device_id_type=MESH)
    for k in range(1, n_seq):
        pl.semaphore_signal(barrier, inc=1, device_id=(me, (seq + k) % n_seq), device_id_type=MESH)

    dest = dst[...]
    steps = lax.broadcasted_iota(jnp.int32, (n, tok), 0)
    owners = jnp.sum((dest >= (steps + 1) * tok).astype(jnp.int32), axis=0, keepdims=True)
    places = dest - owners * tok
    shift = owners - me
    shift = jnp.where(shift < 0, shift + n, shift)
    matches = (steps == shift).astype(F32)
    before = lax.broadcasted_iota(jnp.int32, (tok, tok), 0) <= lax.broadcasted_iota(jnp.int32, (tok, tok), 1)
    counted = jnp.dot(matches.astype(BF16), before.astype(F32).astype(BF16), preferred_element_type=F32)
    slots = jnp.sum(matches * counted, axis=0, keepdims=True).astype(jnp.int32) - 1
    flat = shift * cap + slots
    chosen = (lax.broadcasted_iota(jnp.int32, (n * cap, tok), 0) == flat).astype(F32).astype(BF16)
    named = jnp.broadcast_to((places + 1).astype(F32), (8, tok)).astype(BF16)
    lab_out[...] = lax.dot_general(named, chosen, (((1,), (1,)), ((), ())), preferred_element_type=F32)

    def column(c):
        return pl.ds(*pieces[c])

    def fill(c):
        moved = jnp.dot(chosen, src[0, :, column(c)], preferred_element_type=F32).astype(BF16)
        outbox[:, column(c)] = moved
        inbox[0:cap, column(c)] = moved[0:cap]

    def label_copy(k):
        return remote(lab_out, lab_in.at[k], lab_send.at[k], lab_recv.at[k], ((me + k) % n, seq))

    def dispatch_copy(c, k):
        block = pl.ds(k * cap, cap)
        return remote(
            outbox.at[block, column(c)], inbox.at[block, column(c)], disp_send.at[c, k], disp_recv.at[c, k],
            ((me + k) % n, seq),
        )

    def token_copy(c, d, at_y):
        place = packed.at[at_y, my_c, :, column(c)]
        return remote(place, place, tok_send.at[c, d], tok_recv.at[c, d], on_y(d) if d else sib)

    def token_forward(c, d, at_c):
        place = packed.at[(my_y - d) % rows_y, at_c, :, column(c)]
        return remote(place, place, tokf_send.at[c, d], tokf_recv.at[c, d], sib)

    def weight_copy(c, d):
        place = w_all.at[my_y, my_c, :, column(c)]
        return remote(place, place, w_send.at[c, d], w_recv.at[c, d], on_y(d) if d else sib)

    def weight_forward(c, d, at_c):
        place = w_all.at[(my_y - d) % rows_y, at_c, :, column(c)]
        return remote(place, place, wf_send.at[c, d], wf_recv.at[c, d], sib)

    fill(0)
    pl.semaphore_wait(barrier, n - 1 + n_seq - 1)
    for k in range(1, n):
        label_copy(k).start()
    for k in range(1, n):
        dispatch_copy(0, k).start()

    def send_weights(c):
        for d in range(1, rows_y):
            weight_copy(c, d).start()
        weight_copy(c, 0).start()

    def forward_weights(c):
        for d in range(1, rows_y):
            weight_copy(c, d).wait_recv()
            weight_forward(c, d, my_c).start()

    load_out.wait()
    for c in range(len(pieces)):
        send_weights(c)
    for c in range(1, len(pieces)):
        fill(c)

    doc_row = doc[...].astype(F32)
    doc_col[...] = jnp.broadcast_to(doc_row, (128, length)).T.reshape(doc_col.shape)

    lane = lax.broadcasted_iota(jnp.int32, (1, n * cap), 1)
    label = jnp.where(lane < cap, lab_out[0:1, :], 0.0)
    for k in range(1, n):
        label_copy(k).wait_recv()
        label = jnp.where((lane >= k * cap) & (lane < (k + 1) * cap), lab_in[k, 0:1, :], label)
    rows = lax.broadcasted_iota(jnp.int32, (tok, n * cap), 0) + 1
    placing = (rows.astype(F32) == label).astype(F32).astype(BF16)

    def project(c, at_y):
        block = packed[at_y, :, :, column(c)].reshape(CORES * tok, pieces[c][1])
        for j in range(3):
            part = lax.dot_general(
                block, wqkv[j, :, column(c)], (((1,), (1,)), ((), ())), preferred_element_type=F32
            )
            if c:
                part = part + acc[j, at_y]
            if c < len(pieces) - 1:
                acc[j, at_y] = part
            else:
                qkv[j, at_y] = part.astype(BF16).reshape(CORES, tok, group)

    def consume(c):
        for d in range(1, rows_y):
            token_copy(c, d, (my_y - d) % rows_y).wait_recv()
            token_forward(c, d, my_c).start()
        token_copy(c, 0, my_y).wait_recv()
        project(c, my_y)
        for d in range(1, rows_y):
            token_forward(c, d, 1 - my_c).wait_recv()
            project(c, (my_y - d) % rows_y)

    load_qkv.wait()
    for c in range(len(pieces)):
        for k in range(1, n):
            dispatch_copy(c, k).wait_send()
            if c + 1 < len(pieces):
                dispatch_copy(c + 1, k).start()
        for k in range(1, n):
            dispatch_copy(c, k).wait_recv()
        packed[my_y, my_c, :, column(c)] = jnp.dot(
            placing, inbox[:, column(c)], preferred_element_type=F32
        ).astype(BF16)
        for d in range(1, rows_y):
            token_copy(c, d, my_y).start()
        token_copy(c, 0, my_y).start()
        if c:
            consume(c - 1)
            forward_weights(c - 1)
    consume(len(pieces) - 1)

    factor = math.log2(math.e) / math.sqrt(HD)

    def attended_copy(i, at_c, to):
        return remote(
            att_out.at[i, at_c], att_in.at[i, my_c], att_send.at[i, at_c], att_recv.at[i, my_c], to
        )

    def arrival(i, at_c):
        place = att_in.at[i, at_c]
        return remote(place, place, att_send.at[i, at_c], att_recv.at[i, at_c], sib)

    def attend(i, carry):
        at_y = (my_y + i + 1) % rows_y
        same = doc_col[at_y][:, 0:1] == doc_row
        att_acc[...] = jnp.zeros_like(att_acc)
        for h in range(heads):
            lower, upper = head_window(h, group)
            lanes = lax.broadcasted_iota(jnp.int32, (1, upper - lower), 1) + lower
            mine = (lanes >= h * HD) & (lanes < (h + 1) * HD)
            query = qkv[0, at_y, :, :, lower:upper].reshape(CORES * tok, upper - lower)
            query = jnp.where(mine, query.astype(F32), 0.0).astype(BF16)
            keys = qkv[1, :, :, :, lower:upper].reshape(length, upper - lower)
            values = qkv[2, :, :, :, lower:upper].reshape(length, upper - lower)
            scores = lax.dot_general(query, keys, (((1,), (1,)), ((), ())), preferred_element_type=F32)
            scores = jnp.where(same, scores, -jnp.inf)
            expo = jnp.exp2((scores - jnp.max(scores, axis=1, keepdims=True)) * factor)
            total = jnp.sum(expo, axis=1, keepdims=True)
            mixed = jnp.dot(expo.astype(BF16), values, preferred_element_type=F32) / total
            att_acc[:, lower:upper] += jnp.where(mine, mixed, 0.0)
        att_out[i] = att_acc[...].astype(BF16).reshape(CORES, tok, group)

        @pl.when(i < rows_y - 1)
        def _():
            for at_c in range(CORES):
                attended_copy(i, at_c, (me, at_y * CORES + at_c)).start()

        return carry

    lax.fori_loop(0, rows_y, attend, 0)
    last = rows_y - 1
    attended_copy(last, 1 - my_c, sib).start()
    forward_weights(len(pieces) - 1)

    def mixed_out(rows, at_y, at_c):
        return jnp.dot(rows, w_all[at_y, at_c], preferred_element_type=F32)

    total = mixed_out(att_out[last, my_c], my_y, my_c)
    for c in range(len(pieces)):
        weight_copy(c, 0).wait_recv()
        for d in range(1, rows_y):
            weight_forward(c, d, 1 - my_c).wait_recv()
    for i in range(rows_y - 1):
        for at_c in range(CORES):
            arrival(i, at_c).wait_recv()
            total = total + mixed_out(att_in[i, at_c], (my_y - i - 1) % rows_y, at_c)
    arrival(last, 1 - my_c).wait_recv()
    total = total + mixed_out(att_in[last, 1 - my_c], my_y, 1 - my_c)
    out[0] = total.astype(BF16)

    for k in range(1, n):
        label_copy(k).wait_send()
    for c in range(len(pieces)):
        for d in range(rows_y):
            token_copy(c, d, my_y).wait_send()
            weight_copy(c, d).wait_send()
            if d:
                token_forward(c, d, my_c).wait_send()
                weight_forward(c, d, my_c).wait_send()
    for i in range(rows_y - 1):
        for at_c in range(CORES):
            attended_copy(i, at_c, sib).wait_send()
    attended_copy(last, 1 - my_c, sib).wait_send()


def body(source, destination, doc_ids, w_qkv, w_out):
    n = lax.axis_size("pack")
    n_seq = lax.axis_size("seq")
    rows_y = n_seq // CORES
    tok, width = source.shape[1:]
    group = w_out.shape[0]
    length = doc_ids.shape[1]
    cap = -(-(2 * tok // n) // 16) * 16
    tiles = width // 128
    ends = [0, tiles - tiles * 5 // 9, tiles - tiles * 2 // 9, tiles]
    pieces = [(start * 128, (end - start) * 128) for start, end in zip(ends, ends[1:])]
    parts = len(pieces)
    dma = pltpu.SemaphoreType.DMA
    vmem = pl.BlockSpec(memory_space=pltpu.VMEM)
    return pl.pallas_call(
        functools.partial(kernel, n, rows_y, cap, pieces),
        out_shape=jax.ShapeDtypeStruct((1, tok, width), BF16),
        in_specs=[vmem] * 3 + [pl.BlockSpec(memory_space=pl.ANY)] * 2,
        out_specs=vmem,
        scratch_shapes=[
            pltpu.VMEM((3, group, width), BF16),
            pltpu.VMEM((n * cap, width), BF16),
            pltpu.VMEM((n * cap, width), BF16),
            pltpu.VMEM((8, n * cap), F32),
            pltpu.VMEM((n, 8, n * cap), F32),
            pltpu.VMEM((rows_y, CORES, tok, width), BF16),
            pltpu.VMEM((3, rows_y, CORES * tok, group), F32),
            pltpu.VMEM((3, rows_y, CORES, tok, group), BF16),
            pltpu.VMEM((rows_y, CORES * tok, 128), F32),
            pltpu.VMEM((CORES * tok, group), F32),
            pltpu.VMEM((rows_y, CORES, tok, group), BF16),
            pltpu.VMEM((rows_y, CORES, tok, group), BF16),
            pltpu.VMEM((rows_y, CORES, group, width), BF16),
            dma((parts, n)), dma((parts, n)), dma((n,)), dma((n,)),
            dma((parts, rows_y)), dma((parts, rows_y)), dma((parts, rows_y)), dma((parts, rows_y)),
            dma((parts, rows_y)), dma((parts, rows_y)), dma((parts, rows_y)), dma((parts, rows_y)),
            dma((rows_y, CORES)), dma((rows_y, CORES)), dma((2,)),
        ],
        compiler_params=pltpu.CompilerParams(
            collective_id=0, has_side_effects=True, vmem_limit_bytes=56 * 1024 * 1024
        ),
        cost_estimate=pl.CostEstimate(flops=4_000_000_000, bytes_accessed=4_000_000, transcendentals=2_400_000),
    )(source, destination, doc_ids, jnp.swapaxes(w_qkv, 1, 2), w_out)


def solution(mesh):
    placed = (
        P("seq", "pack", None),
        P("seq", "pack"),
        P("pack", None),
        P(None, None, "seq"),
        P("seq", None),
    )
    return jax.shard_map(
        body, mesh=mesh, in_specs=placed, out_specs=P("pack", "seq", None), check_vma=False
    )
```

```python
import functools
import math

import jax
import jax.numpy as jnp
from jax import lax
from jax.experimental import pallas as pl
from jax.experimental.pallas import tpu as pltpu
from jax.sharding import PartitionSpec as P

HD = 72
CORES = 2
MESH = pl.DeviceIdType.MESH
F32 = jnp.float32
BF16 = jnp.bfloat16


def head_window(head, group):
    lower = head * HD // 128 * 128
    upper = min(-(-(head + 1) * HD // 128) * 128, group)
    return lower, upper


def kernel(
    n, rows_y, cap, pieces,
    src, dst, doc, wqkv_hbm, wout_hbm, out,
    wqkv, outbox, inbox, lab_out, lab_in, packed, acc, qkv, doc_col, bias, att_acc, att_out, att_in, w_all,
    disp_send, disp_recv, lab_send, lab_recv,
    tok_send, tok_recv, tokf_send, tokf_recv,
    w_send, w_recv, wf_send, wf_recv, att_send, att_recv, load_sem,
):
    n_seq = rows_y * CORES
    tok = src.shape[1]
    group = wout_hbm.shape[0]
    length = doc.shape[1]
    heads = group // HD
    me = lax.axis_index("pack")
    seq = lax.axis_index("seq")
    my_y, my_c = seq // CORES, seq % CORES
    sib = (me, my_y * CORES + 1 - my_c)

    def on_y(d):
        return (me, (my_y + d) % rows_y * CORES + my_c)

    def remote(source, target, ss, rs, device):
        return pltpu.make_async_remote_copy(
            src_ref=source, dst_ref=target, send_sem=ss, recv_sem=rs,
            device_id=device, device_id_type=MESH,
        )

    load_qkv = pltpu.make_async_copy(wqkv_hbm, wqkv, load_sem.at[0])
    load_out = pltpu.make_async_copy(wout_hbm, w_all.at[my_y, my_c], load_sem.at[1])
    load_out.start()
    load_qkv.start()

    barrier = pltpu.get_barrier_semaphore()
    for k in range(1, n):
        pl.semaphore_signal(barrier, inc=1, device_id=((me + k) % n, seq), device_id_type=MESH)
    for k in range(1, n_seq):
        pl.semaphore_signal(barrier, inc=1, device_id=(me, (seq + k) % n_seq), device_id_type=MESH)

    dest = dst[...]
    steps = lax.broadcasted_iota(jnp.int32, (n, tok), 0)
    owners = jnp.sum((dest >= (steps + 1) * tok).astype(jnp.int32), axis=0, keepdims=True)
    places = dest - owners * tok
    shift = owners - me
    shift = jnp.where(shift < 0, shift + n, shift)
    matches = (steps == shift).astype(F32)
    before = lax.broadcasted_iota(jnp.int32, (tok, tok), 0) <= lax.broadcasted_iota(jnp.int32, (tok, tok), 1)
    counted = jnp.dot(matches.astype(BF16), before.astype(F32).astype(BF16), preferred_element_type=F32)
    slots = jnp.sum(matches * counted, axis=0, keepdims=True).astype(jnp.int32) - 1
    flat = shift * cap + slots
    chosen = (lax.broadcasted_iota(jnp.int32, (n * cap, tok), 0) == flat).astype(F32).astype(BF16)
    named = jnp.broadcast_to((places + 1).astype(F32), (8, tok)).astype(BF16)
    lab_out[...] = lax.dot_general(named, chosen, (((1,), (1,)), ((), ())), preferred_element_type=F32)

    def column(c):
        return pl.ds(*pieces[c])

    def fill(c):
        moved = jnp.dot(chosen, src[0, :, column(c)], preferred_element_type=F32).astype(BF16)
        outbox[:, column(c)] = moved
        inbox[0:cap, column(c)] = moved[0:cap]

    def label_copy(k):
        return remote(lab_out, lab_in.at[k], lab_send.at[k], lab_recv.at[k], ((me + k) % n, seq))

    def dispatch_copy(c, k):
        block = pl.ds(k * cap, cap)
        return remote(
            outbox.at[block, column(c)], inbox.at[block, column(c)], disp_send.at[c, k], disp_recv.at[c, k],
            ((me + k) % n, seq),
        )

    def token_copy(c, d, at_y):
        place = packed.at[at_y, my_c, :, column(c)]
        return remote(place, place, tok_send.at[c, d], tok_recv.at[c, d], on_y(d) if d else sib)

    def token_forward(c, d, at_c):
        place = packed.at[(my_y - d) % rows_y, at_c, :, column(c)]
        return remote(place, place, tokf_send.at[c, d], tokf_recv.at[c, d], sib)

    def weight_copy(c, d):
        place = w_all.at[my_y, my_c, :, column(c)]
        return remote(place, place, w_send.at[c, d], w_recv.at[c, d], on_y(d) if d else sib)

    def weight_forward(c, d, at_c):
        place = w_all.at[(my_y - d) % rows_y, at_c, :, column(c)]
        return remote(place, place, wf_send.at[c, d], wf_recv.at[c, d], sib)

    fill(0)
    pl.semaphore_wait(barrier, n - 1 + n_seq - 1)
    for k in range(1, n):
        label_copy(k).start()
    for c in range(len(pieces)):
        if c:
            fill(c)
        for k in range(1, n):
            dispatch_copy(c, k).start()

    def send_weights(c):
        for d in range(1, rows_y):
            weight_copy(c, d).start()
        weight_copy(c, 0).start()

    def forward_weights(c):
        for d in range(1, rows_y):
            weight_copy(c, d).wait_recv()
            weight_forward(c, d, my_c).start()

    load_out.wait()
    for c in range(len(pieces)):
        send_weights(c)

    doc_row = doc[...].astype(F32)
    doc_col[...] = jnp.broadcast_to(doc_row, (128, length)).T.reshape(doc_col.shape)

    lane = lax.broadcasted_iota(jnp.int32, (1, n * cap), 1)
    label = jnp.where(lane < cap, lab_out[0:1, :], 0.0)
    for k in range(1, n):
        label_copy(k).wait_recv()
        label = jnp.where((lane >= k * cap) & (lane < (k + 1) * cap), lab_in[k, 0:1, :], label)
    rows = lax.broadcasted_iota(jnp.int32, (tok, n * cap), 0) + 1
    placing = (rows.astype(F32) == label).astype(F32).astype(BF16)

    factor = math.log2(math.e) / math.sqrt(HD)

    def project(c, at_y):
        block = packed[at_y, :, :, column(c)].reshape(CORES * tok, pieces[c][1])
        for j in range(3):
            part = lax.dot_general(
                block, wqkv[j, :, column(c)], (((1,), (1,)), ((), ())), preferred_element_type=F32
            )
            if c:
                part = part + acc[j, at_y]
            if c < len(pieces) - 1:
                acc[j, at_y] = part
            else:
                if j == 0:
                    part = part * factor
                qkv[j, at_y] = part.astype(BF16).reshape(CORES, tok, group)

    def consume(c):
        for d in range(1, rows_y):
            token_copy(c, d, (my_y - d) % rows_y).wait_recv()
            token_forward(c, d, my_c).start()
        token_copy(c, 0, my_y).wait_recv()
        project(c, my_y)
        for d in range(1, rows_y):
            token_forward(c, d, 1 - my_c).wait_recv()
            project(c, (my_y - d) % rows_y)

    load_qkv.wait()
    for c in range(len(pieces)):
        for k in range(1, n):
            dispatch_copy(c, k).wait_recv()
        packed[my_y, my_c, :, column(c)] = jnp.dot(
            placing, inbox[:, column(c)], preferred_element_type=F32
        ).astype(BF16)
        for d in range(1, rows_y):
            token_copy(c, d, my_y).start()
        token_copy(c, 0, my_y).start()
        if c:
            consume(c - 1)
            forward_weights(c - 1)
    consume(len(pieces) - 1)

    def attended_copy(i, at_c, to):
        return remote(
            att_out.at[i, at_c], att_in.at[i, my_c], att_send.at[i, at_c], att_recv.at[i, my_c], to
        )

    def arrival(i, at_c):
        place = att_in.at[i, at_c]
        return remote(place, place, att_send.at[i, at_c], att_recv.at[i, at_c], sib)

    def attend(i, carry):
        at_y = (my_y + i + 1) % rows_y
        bias[...] = jnp.where(doc_col[at_y][:, 0:1] == doc_row, 0.0, -jnp.inf)
        att_acc[...] = jnp.zeros_like(att_acc)
        for h in range(heads):
            lower, upper = head_window(h, group)
            lanes = lax.broadcasted_iota(jnp.int32, (1, upper - lower), 1) + lower
            mine = (lanes >= h * HD) & (lanes < (h + 1) * HD)
            query = qkv[0, at_y, :, :, lower:upper].reshape(CORES * tok, upper - lower)
            query = jnp.where(mine, query.astype(F32), 0.0).astype(BF16)
            keys = qkv[1, :, :, :, lower:upper].reshape(length, upper - lower)
            values = qkv[2, :, :, :, lower:upper].reshape(length, upper - lower)
            scores = lax.dot_general(query, keys, (((1,), (1,)), ((), ())), preferred_element_type=F32)
            scores = scores + bias[...]
            expo = jnp.exp2(scores - jnp.max(scores, axis=1, keepdims=True))
            share = 1.0 / jnp.sum(expo, axis=1, keepdims=True)
            mixed = jnp.dot(expo.astype(BF16), values, preferred_element_type=F32) * share
            att_acc[:, lower:upper] += jnp.where(mine, mixed, 0.0)
        att_out[i] = att_acc[...].astype(BF16).reshape(CORES, tok, group)

        @pl.when(i < rows_y - 1)
        def _():
            for at_c in range(CORES):
                attended_copy(i, at_c, (me, at_y * CORES + at_c)).start()

        return carry

    lax.fori_loop(0, rows_y, attend, 0)
    last = rows_y - 1
    attended_copy(last, 1 - my_c, sib).start()
    forward_weights(len(pieces) - 1)

    def mixed_out(rows, at_y, at_c):
        return jnp.dot(rows, w_all[at_y, at_c], preferred_element_type=F32)

    total = mixed_out(att_out[last, my_c], my_y, my_c)
    for c in range(len(pieces)):
        weight_copy(c, 0).wait_recv()
        for d in range(1, rows_y):
            weight_forward(c, d, 1 - my_c).wait_recv()
    for i in range(rows_y - 1):
        for at_c in range(CORES):
            arrival(i, at_c).wait_recv()
            total = total + mixed_out(att_in[i, at_c], (my_y - i - 1) % rows_y, at_c)
    arrival(last, 1 - my_c).wait_recv()
    total = total + mixed_out(att_in[last, 1 - my_c], my_y, 1 - my_c)
    out[0] = total.astype(BF16)

    for k in range(1, n):
        label_copy(k).wait_send()
    for c in range(len(pieces)):
        for k in range(1, n):
            dispatch_copy(c, k).wait_send()
        for d in range(rows_y):
            token_copy(c, d, my_y).wait_send()
            weight_copy(c, d).wait_send()
            if d:
                token_forward(c, d, my_c).wait_send()
                weight_forward(c, d, my_c).wait_send()
    for i in range(rows_y - 1):
        for at_c in range(CORES):
            attended_copy(i, at_c, sib).wait_send()
    attended_copy(last, 1 - my_c, sib).wait_send()


def pass_on(given, out):
    out[...] = given[...]


def body(source, destination, doc_ids, w_qkv, w_out):
    n = lax.axis_size("pack")
    n_seq = lax.axis_size("seq")
    rows_y = n_seq // CORES
    tok, width = source.shape[1:]
    group = w_out.shape[0]
    length = doc_ids.shape[1]
    cap = -(-(2 * tok // n) // 16) * 16
    tiles = width // 128
    ends = [0, tiles - tiles * 5 // 9, tiles - tiles * 2 // 9, tiles]
    pieces = [(start * 128, (end - start) * 128) for start, end in zip(ends, ends[1:])]
    parts = len(pieces)
    dma = pltpu.SemaphoreType.DMA
    vmem = pl.BlockSpec(memory_space=pltpu.VMEM)
    result = pl.pallas_call(
        functools.partial(kernel, n, rows_y, cap, pieces),
        out_shape=jax.ShapeDtypeStruct((1, tok, width), BF16),
        in_specs=[vmem] * 3 + [pl.BlockSpec(memory_space=pl.ANY)] * 2,
        out_specs=vmem,
        scratch_shapes=[
            pltpu.VMEM((3, group, width), BF16),
            pltpu.VMEM((n * cap, width), BF16),
            pltpu.VMEM((n * cap, width), BF16),
            pltpu.VMEM((8, n * cap), F32),
            pltpu.VMEM((n, 8, n * cap), F32),
            pltpu.VMEM((rows_y, CORES, tok, width), BF16),
            pltpu.VMEM((3, rows_y, CORES * tok, group), F32),
            pltpu.VMEM((3, rows_y, CORES, tok, group), BF16),
            pltpu.VMEM((rows_y, CORES * tok, 128), F32),
            pltpu.VMEM((CORES * tok, length), F32),
            pltpu.VMEM((CORES * tok, group), F32),
            pltpu.VMEM((rows_y, CORES, tok, group), BF16),
            pltpu.VMEM((rows_y, CORES, tok, group), BF16),
            pltpu.VMEM((rows_y, CORES, group, width), BF16),
            dma((parts, n)), dma((parts, n)), dma((n,)), dma((n,)),
            dma((parts, rows_y)), dma((parts, rows_y)), dma((parts, rows_y)), dma((parts, rows_y)),
            dma((parts, rows_y)), dma((parts, rows_y)), dma((parts, rows_y)), dma((parts, rows_y)),
            dma((rows_y, CORES)), dma((rows_y, CORES)), dma((2,)),
        ],
        compiler_params=pltpu.CompilerParams(
            collective_id=0, has_side_effects=True, vmem_limit_bytes=56 * 1024 * 1024
        ),
        cost_estimate=pl.CostEstimate(flops=4_000_000_000, bytes_accessed=4_000_000, transcendentals=2_400_000),
    )(source, destination, doc_ids, jnp.swapaxes(w_qkv, 1, 2), w_out)
    return pl.pallas_call(
        pass_on, out_shape=jax.ShapeDtypeStruct(result.shape, BF16), in_specs=[vmem], out_specs=vmem
    )(result)


def solution(mesh):
    placed = (
        P("seq", "pack", None),
        P("seq", "pack"),
        P("pack", None),
        P(None, None, "seq"),
        P("seq", None),
    )
    return jax.shard_map(
        body, mesh=mesh, in_specs=placed, out_specs=P("pack", "seq", None), check_vma=False
    )
```

```python
import functools
import math

import jax
import jax.numpy as jnp
from jax import lax
from jax.experimental import pallas as pl
from jax.experimental.pallas import tpu as pltpu
from jax.sharding import PartitionSpec as P

HD = 72
CORES = 2
MESH = pl.DeviceIdType.MESH
F32 = jnp.float32
BF16 = jnp.bfloat16


def head_window(head, group):
    lower = head * HD // 128 * 128
    upper = min(-(-(head + 1) * HD // 128) * 128, group)
    return lower, upper


def kernel(
    n, rows_y, cap, pieces,
    src, dst, doc, wqkv_hbm, wout_hbm, out,
    wqkv, outbox, inbox, lab_out, lab_in, packed, acc, qkv, doc_col, bias, att_acc, att_out, att_in, rest_out, rest_in, w_all,
    disp_send, disp_recv, lab_send, lab_recv,
    tok_send, tok_recv, tokf_send, tokf_recv,
    w_send, w_recv, wf_send, wf_recv, att_send, att_recv, load_sem,
):
    n_seq = rows_y * CORES
    tok = src.shape[1]
    group = wout_hbm.shape[0]
    length = doc.shape[1]
    heads = group // HD
    me = lax.axis_index("pack")
    seq = lax.axis_index("seq")
    my_y, my_c = seq // CORES, seq % CORES
    sib = (me, my_y * CORES + 1 - my_c)

    def on_y(d):
        return (me, (my_y + d) % rows_y * CORES + my_c)

    def remote(source, target, ss, rs, device):
        return pltpu.make_async_remote_copy(
            src_ref=source, dst_ref=target, send_sem=ss, recv_sem=rs,
            device_id=device, device_id_type=MESH,
        )

    load_qkv = pltpu.make_async_copy(wqkv_hbm, wqkv, load_sem.at[0])
    load_out = pltpu.make_async_copy(wout_hbm, w_all.at[my_y, my_c], load_sem.at[1])
    load_out.start()
    load_qkv.start()

    barrier = pltpu.get_barrier_semaphore()
    for k in range(1, n):
        pl.semaphore_signal(barrier, inc=1, device_id=((me + k) % n, seq), device_id_type=MESH)
    for k in range(1, n_seq):
        pl.semaphore_signal(barrier, inc=1, device_id=(me, (seq + k) % n_seq), device_id_type=MESH)

    dest = dst[...]
    steps = lax.broadcasted_iota(jnp.int32, (n, tok), 0)
    owners = jnp.sum((dest >= (steps + 1) * tok).astype(jnp.int32), axis=0, keepdims=True)
    places = dest - owners * tok
    shift = owners - me
    shift = jnp.where(shift < 0, shift + n, shift)
    matches = (steps == shift).astype(F32)
    before = lax.broadcasted_iota(jnp.int32, (tok, tok), 0) <= lax.broadcasted_iota(jnp.int32, (tok, tok), 1)
    counted = jnp.dot(matches.astype(BF16), before.astype(F32).astype(BF16), preferred_element_type=F32)
    slots = jnp.sum(matches * counted, axis=0, keepdims=True).astype(jnp.int32) - 1
    flat = shift * cap + slots
    chosen = (lax.broadcasted_iota(jnp.int32, (n * cap, tok), 0) == flat).astype(F32).astype(BF16)
    named = jnp.broadcast_to((places + 1).astype(F32), (8, tok)).astype(BF16)
    lab_out[...] = lax.dot_general(named, chosen, (((1,), (1,)), ((), ())), preferred_element_type=F32)

    def column(c):
        return pl.ds(*pieces[c])

    def fill(c):
        moved = jnp.dot(chosen, src[0, :, column(c)], preferred_element_type=F32).astype(BF16)
        outbox[:, column(c)] = moved
        inbox[0:cap, column(c)] = moved[0:cap]

    def label_copy(k):
        return remote(lab_out, lab_in.at[k], lab_send.at[k], lab_recv.at[k], ((me + k) % n, seq))

    def dispatch_copy(c, k):
        block = pl.ds(k * cap, cap)
        return remote(
            outbox.at[block, column(c)], inbox.at[block, column(c)], disp_send.at[c, k], disp_recv.at[c, k],
            ((me + k) % n, seq),
        )

    def token_copy(c, d, at_y):
        place = packed.at[at_y, my_c, :, column(c)]
        return remote(place, place, tok_send.at[c, d], tok_recv.at[c, d], on_y(d) if d else sib)

    def token_forward(c, d, at_c):
        place = packed.at[(my_y - d) % rows_y, at_c, :, column(c)]
        return remote(place, place, tokf_send.at[c, d], tokf_recv.at[c, d], sib)

    def weight_copy(c, d):
        place = w_all.at[my_y, my_c, :, column(c)]
        return remote(place, place, w_send.at[c, d], w_recv.at[c, d], on_y(d) if d else sib)

    def weight_forward(c, d, at_c):
        place = w_all.at[(my_y - d) % rows_y, at_c, :, column(c)]
        return remote(place, place, wf_send.at[c, d], wf_recv.at[c, d], sib)

    fill(0)
    pl.semaphore_wait(barrier, n - 1 + n_seq - 1)
    for k in range(1, n):
        label_copy(k).start()
    for c in range(len(pieces)):
        if c:
            fill(c)
        for k in range(1, n):
            dispatch_copy(c, k).start()

    def send_weights(c):
        for d in range(1, rows_y):
            weight_copy(c, d).start()
        weight_copy(c, 0).start()

    def forward_weights(c):
        for d in range(1, rows_y):
            weight_copy(c, d).wait_recv()
            weight_forward(c, d, my_c).start()

    load_out.wait()
    for c in range(len(pieces) - 1):
        send_weights(c)

    doc_row = doc[...].astype(F32)
    doc_col[...] = jnp.broadcast_to(doc_row, (128, length)).T.reshape(doc_col.shape)

    lane = lax.broadcasted_iota(jnp.int32, (1, n * cap), 1)
    label = jnp.where(lane < cap, lab_out[0:1, :], 0.0)
    for k in range(1, n):
        label_copy(k).wait_recv()
        label = jnp.where((lane >= k * cap) & (lane < (k + 1) * cap), lab_in[k, 0:1, :], label)
    rows = lax.broadcasted_iota(jnp.int32, (tok, n * cap), 0) + 1
    placing = (rows.astype(F32) == label).astype(F32).astype(BF16)

    factor = math.log2(math.e) / math.sqrt(HD)

    def project(c, at_y):
        block = packed[at_y, :, :, column(c)].reshape(CORES * tok, pieces[c][1])
        for j in range(3):
            part = lax.dot_general(
                block, wqkv[j, :, column(c)], (((1,), (1,)), ((), ())), preferred_element_type=F32
            )
            if c:
                part = part + acc[j, at_y]
            if c < len(pieces) - 1:
                acc[j, at_y] = part
            else:
                if j == 0:
                    part = part * factor
                qkv[j, at_y] = part.astype(BF16).reshape(CORES, tok, group)

    def consume(c):
        for d in range(1, rows_y):
            token_copy(c, d, (my_y - d) % rows_y).wait_recv()
            token_forward(c, d, my_c).start()
        token_copy(c, 0, my_y).wait_recv()
        project(c, my_y)
        for d in range(1, rows_y):
            token_forward(c, d, 1 - my_c).wait_recv()
            project(c, (my_y - d) % rows_y)

    load_qkv.wait()
    for c in range(len(pieces)):
        for k in range(1, n):
            dispatch_copy(c, k).wait_recv()
        packed[my_y, my_c, :, column(c)] = jnp.dot(
            placing, inbox[:, column(c)], preferred_element_type=F32
        ).astype(BF16)
        for d in range(1, rows_y):
            token_copy(c, d, my_y).start()
        token_copy(c, 0, my_y).start()
        if c:
            consume(c - 1)
            forward_weights(c - 1)
    send_weights(len(pieces) - 1)
    consume(len(pieces) - 1)

    tiles = group // 128
    rest = group - tiles * 128
    fold = tok // rest_out.shape[2]

    def tile(t):
        return pl.ds(t * 128, 128)

    def attended_copy(i, at_c, t, to):
        if t < tiles:
            source, place = att_out.at[i, at_c, :, tile(t)], att_in.at[i, my_c, :, tile(t)]
        else:
            source, place = rest_out.at[i, at_c], rest_in.at[i, my_c]
        return remote(source, place, att_send.at[i, at_c, t], att_recv.at[i, my_c, t], to)

    def arrived(i, at_c):
        for t in range(tiles + 1):
            place = att_in.at[i, at_c, :, tile(t)] if t < tiles else rest_in.at[i, at_c]
            remote(place, place, att_send.at[i, at_c, t], att_recv.at[i, at_c, t], sib).wait_recv()

    def attend(i, carry):
        at_y = (my_y + i + 1) % rows_y
        bias[...] = jnp.where(doc_col[at_y][:, 0:1] == doc_row, 0.0, -jnp.inf)
        att_acc[...] = jnp.zeros_like(att_acc)
        for h in range(heads):
            lower, upper = head_window(h, group)
            lanes = lax.broadcasted_iota(jnp.int32, (1, upper - lower), 1) + lower
            mine = (lanes >= h * HD) & (lanes < (h + 1) * HD)
            query = qkv[0, at_y, :, :, lower:upper].reshape(CORES * tok, upper - lower)
            query = jnp.where(mine, query.astype(F32), 0.0).astype(BF16)
            keys = qkv[1, :, :, :, lower:upper].reshape(length, upper - lower)
            values = qkv[2, :, :, :, lower:upper].reshape(length, upper - lower)
            scores = lax.dot_general(query, keys, (((1,), (1,)), ((), ())), preferred_element_type=F32)
            scores = scores + bias[...]
            expo = jnp.exp2(scores - jnp.max(scores, axis=1, keepdims=True))
            share = 1.0 / jnp.sum(expo, axis=1, keepdims=True)
            mixed = jnp.dot(expo.astype(BF16), values, preferred_element_type=F32) * share
            att_acc[:, lower:upper] += jnp.where(mine, mixed, 0.0)
            ready = [t for t in range(tiles) if h * HD < (t + 1) * 128 <= (h + 1) * HD]
            for t in ready:
                att_out[i, :, :, tile(t)] = att_acc[:, tile(t)].astype(BF16).reshape(CORES, tok, 128)
            if h == heads - 1:
                spare = att_acc[:, tiles * 128 : group].reshape(CORES, fold, tok // fold, rest)
                spare = jnp.concatenate([spare[:, j] for j in range(fold)], axis=2)
                rest_out[i] = spare.astype(BF16)
                ready = ready + [tiles]

            @pl.when(i < rows_y - 1)
            def _():
                for t in ready:
                    for at_c in range(CORES):
                        attended_copy(i, at_c, t, (me, at_y * CORES + at_c)).start()

        return carry

    lax.fori_loop(0, rows_y, attend, 0)
    last = rows_y - 1
    for t in range(tiles + 1):
        attended_copy(last, 1 - my_c, t, sib).start()
    forward_weights(len(pieces) - 1)

    def mixed_out(rows, spare, at_y, at_c):
        spare = spare.astype(F32)
        spare = jnp.concatenate([spare[:, j * rest : (j + 1) * rest] for j in range(fold)], axis=0)
        product = jnp.dot(
            spare.astype(BF16), w_all[at_y, at_c, tiles * 128 : group, :], preferred_element_type=F32
        )
        if tiles:
            product = product + jnp.dot(
                rows[:, : tiles * 128], w_all[at_y, at_c, : tiles * 128, :], preferred_element_type=F32
            )
        return product

    total = mixed_out(att_out[last, my_c], rest_out[last, my_c], my_y, my_c)
    for c in range(len(pieces)):
        weight_copy(c, 0).wait_recv()
        for d in range(1, rows_y):
            weight_forward(c, d, 1 - my_c).wait_recv()
    for i in range(rows_y - 1):
        for at_c in range(CORES):
            arrived(i, at_c)
            total = total + mixed_out(att_in[i, at_c], rest_in[i, at_c], (my_y - i - 1) % rows_y, at_c)
    arrived(last, 1 - my_c)
    total = total + mixed_out(att_in[last, 1 - my_c], rest_in[last, 1 - my_c], my_y, 1 - my_c)
    out[0] = total.astype(BF16)

    for k in range(1, n):
        label_copy(k).wait_send()
    for c in range(len(pieces)):
        for k in range(1, n):
            dispatch_copy(c, k).wait_send()
        for d in range(rows_y):
            token_copy(c, d, my_y).wait_send()
            weight_copy(c, d).wait_send()
            if d:
                token_forward(c, d, my_c).wait_send()
                weight_forward(c, d, my_c).wait_send()
    for i in range(rows_y - 1):
        for at_c in range(CORES):
            for t in range(tiles + 1):
                attended_copy(i, at_c, t, sib).wait_send()
    for t in range(tiles + 1):
        attended_copy(last, 1 - my_c, t, sib).wait_send()


def pass_on(given, out):
    out[...] = given[...]


def body(source, destination, doc_ids, w_qkv, w_out):
    n = lax.axis_size("pack")
    n_seq = lax.axis_size("seq")
    rows_y = n_seq // CORES
    tok, width = source.shape[1:]
    group = w_out.shape[0]
    length = doc_ids.shape[1]
    cap = -(-(2 * tok // n) // 16) * 16
    tiles = width // 128
    ends = [0, tiles - tiles * 5 // 9, tiles - tiles * 2 // 9, tiles]
    pieces = [(start * 128, (end - start) * 128) for start, end in zip(ends, ends[1:])]
    parts = len(pieces)
    rest = group % 128
    fold = 128 // rest
    dma = pltpu.SemaphoreType.DMA
    vmem = pl.BlockSpec(memory_space=pltpu.VMEM)
    result = pl.pallas_call(
        functools.partial(kernel, n, rows_y, cap, pieces),
        out_shape=jax.ShapeDtypeStruct((1, tok, width), BF16),
        in_specs=[vmem] * 3 + [pl.BlockSpec(memory_space=pl.ANY)] * 2,
        out_specs=vmem,
        scratch_shapes=[
            pltpu.VMEM((3, group, width), BF16),
            pltpu.VMEM((n * cap, width), BF16),
            pltpu.VMEM((n * cap, width), BF16),
            pltpu.VMEM((8, n * cap), F32),
            pltpu.VMEM((n, 8, n * cap), F32),
            pltpu.VMEM((rows_y, CORES, tok, width), BF16),
            pltpu.VMEM((3, rows_y, CORES * tok, group), F32),
            pltpu.VMEM((3, rows_y, CORES, tok, group), BF16),
            pltpu.VMEM((rows_y, CORES * tok, 128), F32),
            pltpu.VMEM((CORES * tok, length), F32),
            pltpu.VMEM((CORES * tok, group), F32),
            pltpu.VMEM((rows_y, CORES, tok, group), BF16),
            pltpu.VMEM((rows_y, CORES, tok, group), BF16),
            pltpu.VMEM((rows_y, CORES, tok // fold, rest * fold), BF16),
            pltpu.VMEM((rows_y, CORES, tok // fold, rest * fold), BF16),
            pltpu.VMEM((rows_y, CORES, group, width), BF16),
            dma((parts, n)), dma((parts, n)), dma((n,)), dma((n,)),
            dma((parts, rows_y)), dma((parts, rows_y)), dma((parts, rows_y)), dma((parts, rows_y)),
            dma((parts, rows_y)), dma((parts, rows_y)), dma((parts, rows_y)), dma((parts, rows_y)),
            dma((rows_y, CORES, group // 128 + 1)), dma((rows_y, CORES, group // 128 + 1)), dma((2,)),
        ],
        compiler_params=pltpu.CompilerParams(
            collective_id=0, has_side_effects=True, vmem_limit_bytes=56 * 1024 * 1024
        ),
        cost_estimate=pl.CostEstimate(flops=4_000_000_000, bytes_accessed=4_000_000, transcendentals=2_400_000),
    )(source, destination, doc_ids, jnp.swapaxes(w_qkv, 1, 2), w_out)
    return pl.pallas_call(
        pass_on, out_shape=jax.ShapeDtypeStruct(result.shape, BF16), in_specs=[vmem], out_specs=vmem
    )(result)


def solution(mesh):
    placed = (
        P("seq", "pack", None),
        P("seq", "pack"),
        P("pack", None),
        P(None, None, "seq"),
        P("seq", None),
    )
    return jax.shard_map(
        body, mesh=mesh, in_specs=placed, out_specs=P("pack", "seq", None), check_vma=False
    )
```

```python
import functools
import math

import jax
import jax.numpy as jnp
from jax import lax
from jax.experimental import pallas as pl
from jax.experimental.pallas import tpu as pltpu
from jax.sharding import PartitionSpec as P

HD = 72
CORES = 2
AHEAD = 2
MESH = pl.DeviceIdType.MESH
F32 = jnp.float32
BF16 = jnp.bfloat16


def head_window(head, group):
    lower = head * HD // 128 * 128
    upper = min(-(-(head + 1) * HD // 128) * 128, group)
    return lower, upper


def kernel(
    n, rows_y, cap, pieces,
    src, dst, doc, wqkv_hbm, wout_hbm, out,
    wqkv, outbox, inbox, lab_out, lab_in, packed, acc, qkv, doc_col, bias, att_acc, att_out, att_in, rest_out, rest_in, w_all,
    disp_send, disp_recv, lab_send, lab_recv,
    tok_send, tok_recv, tokf_send, tokf_recv,
    w_send, w_recv, wf_send, wf_recv, att_send, att_recv, load_sem,
):
    n_seq = rows_y * CORES
    early = len(pieces) * 3 // 5
    tok = src.shape[1]
    group = wout_hbm.shape[0]
    length = doc.shape[1]
    heads = group // HD
    me = lax.axis_index("pack")
    seq = lax.axis_index("seq")
    my_y, my_c = seq // CORES, seq % CORES
    sib = (me, my_y * CORES + 1 - my_c)

    def on_y(d):
        return (me, (my_y + d) % rows_y * CORES + my_c)

    def remote(source, target, ss, rs, device):
        return pltpu.make_async_remote_copy(
            src_ref=source, dst_ref=target, send_sem=ss, recv_sem=rs,
            device_id=device, device_id_type=MESH,
        )

    load_qkv = pltpu.make_async_copy(wqkv_hbm, wqkv, load_sem.at[0])
    load_out = pltpu.make_async_copy(wout_hbm, w_all.at[my_y, my_c], load_sem.at[1])
    load_out.start()
    load_qkv.start()

    barrier = pltpu.get_barrier_semaphore()
    for k in range(1, n):
        pl.semaphore_signal(barrier, inc=1, device_id=((me + k) % n, seq), device_id_type=MESH)
    for k in range(1, n_seq):
        pl.semaphore_signal(barrier, inc=1, device_id=(me, (seq + k) % n_seq), device_id_type=MESH)

    dest = dst[...]
    steps = lax.broadcasted_iota(jnp.int32, (n, tok), 0)
    owners = jnp.sum((dest >= (steps + 1) * tok).astype(jnp.int32), axis=0, keepdims=True)
    places = dest - owners * tok
    shift = owners - me
    shift = jnp.where(shift < 0, shift + n, shift)
    matches = (steps == shift).astype(F32)
    before = lax.broadcasted_iota(jnp.int32, (tok, tok), 0) <= lax.broadcasted_iota(jnp.int32, (tok, tok), 1)
    counted = jnp.dot(matches.astype(BF16), before.astype(F32).astype(BF16), preferred_element_type=F32)
    slots = jnp.sum(matches * counted, axis=0, keepdims=True).astype(jnp.int32) - 1
    flat = shift * cap + slots
    chosen = (lax.broadcasted_iota(jnp.int32, (n * cap, tok), 0) == flat).astype(F32).astype(BF16)
    named = jnp.broadcast_to((places + 1).astype(F32), (8, tok)).astype(BF16)
    lab_out[...] = lax.dot_general(named, chosen, (((1,), (1,)), ((), ())), preferred_element_type=F32)

    def column(c):
        return pl.ds(*pieces[c])

    def fill(c):
        moved = jnp.dot(chosen, src[0, :, column(c)], preferred_element_type=F32).astype(BF16)
        outbox[:, column(c)] = moved
        inbox[0:cap, column(c)] = moved[0:cap]

    def label_copy(k):
        return remote(lab_out, lab_in.at[k], lab_send.at[k], lab_recv.at[k], ((me + k) % n, seq))

    def dispatch_copy(c, k):
        block = pl.ds(k * cap, cap)
        return remote(
            outbox.at[block, column(c)], inbox.at[block, column(c)], disp_send.at[c, k], disp_recv.at[c, k],
            ((me + k) % n, seq),
        )

    def token_copy(c, d, at_y):
        place = packed.at[at_y, my_c, :, column(c)]
        return remote(place, place, tok_send.at[c, d], tok_recv.at[c, d], on_y(d) if d else sib)

    def token_forward(c, d, at_c):
        place = packed.at[(my_y - d) % rows_y, at_c, :, column(c)]
        return remote(place, place, tokf_send.at[c, d], tokf_recv.at[c, d], sib)

    def weight_copy(c, d):
        place = w_all.at[my_y, my_c, :, column(c)]
        return remote(place, place, w_send.at[c, d], w_recv.at[c, d], on_y(d) if d else sib)

    def weight_forward(c, d, at_c):
        place = w_all.at[(my_y - d) % rows_y, at_c, :, column(c)]
        return remote(place, place, wf_send.at[c, d], wf_recv.at[c, d], sib)

    fill(0)
    pl.semaphore_wait(barrier, n - 1 + n_seq - 1)
    for k in range(1, n):
        label_copy(k).start()
    for c in range(AHEAD):
        if c:
            fill(c)
        for k in range(1, n):
            dispatch_copy(c, k).start()

    def send_weights(c):
        for d in range(1, rows_y):
            weight_copy(c, d).start()
        weight_copy(c, 0).start()

    def forward_weights(c):
        for d in range(1, rows_y):
            weight_copy(c, d).wait_recv()
            weight_forward(c, d, my_c).start()

    load_out.wait()
    for c in range(early):
        send_weights(c)
    for c in range(AHEAD, len(pieces)):
        fill(c)

    doc_row = doc[...].astype(F32)
    doc_col[...] = jnp.broadcast_to(doc_row, (128, length)).T.reshape(doc_col.shape)

    lane = lax.broadcasted_iota(jnp.int32, (1, n * cap), 1)
    label = jnp.where(lane < cap, lab_out[0:1, :], 0.0)
    for k in range(1, n):
        label_copy(k).wait_recv()
        label = jnp.where((lane >= k * cap) & (lane < (k + 1) * cap), lab_in[k, 0:1, :], label)
    rows = lax.broadcasted_iota(jnp.int32, (tok, n * cap), 0) + 1
    placing = (rows.astype(F32) == label).astype(F32).astype(BF16)

    factor = math.log2(math.e) / math.sqrt(HD)

    def project(c, at_y):
        block = packed[at_y, :, :, column(c)].reshape(CORES * tok, pieces[c][1])
        for j in range(3):
            part = lax.dot_general(
                block, wqkv[j, :, column(c)], (((1,), (1,)), ((), ())), preferred_element_type=F32
            )
            if c:
                part = part + acc[j, at_y]
            if c < len(pieces) - 1:
                acc[j, at_y] = part
            else:
                if j == 0:
                    part = part * factor
                qkv[j, at_y] = part.astype(BF16).reshape(CORES, tok, group)

    def consume(c):
        for d in range(1, rows_y):
            token_copy(c, d, (my_y - d) % rows_y).wait_recv()
            token_forward(c, d, my_c).start()
        token_copy(c, 0, my_y).wait_recv()
        project(c, my_y)
        for d in range(1, rows_y):
            token_forward(c, d, 1 - my_c).wait_recv()
            project(c, (my_y - d) % rows_y)

    load_qkv.wait()
    for c in range(len(pieces)):
        for k in range(1, n):
            dispatch_copy(c, k).wait_send()
            if c + AHEAD < len(pieces):
                dispatch_copy(c + AHEAD, k).start()
        for k in range(1, n):
            dispatch_copy(c, k).wait_recv()
        packed[my_y, my_c, :, column(c)] = jnp.dot(
            placing, inbox[:, column(c)], preferred_element_type=F32
        ).astype(BF16)
        for d in range(1, rows_y):
            token_copy(c, d, my_y).start()
        token_copy(c, 0, my_y).start()
        if c:
            consume(c - 1)
            if c - 1 < early:
                forward_weights(c - 1)
    for c in range(early, len(pieces)):
        send_weights(c)
    consume(len(pieces) - 1)

    tiles = group // 128
    rest = group - tiles * 128
    fold = tok // rest_out.shape[2]

    def tile(t):
        return pl.ds(t * 128, 128)

    def attended_copy(i, at_c, t, to):
        if t < tiles:
            source, place = att_out.at[i, at_c, :, tile(t)], att_in.at[i, my_c, :, tile(t)]
        else:
            source, place = rest_out.at[i, at_c], rest_in.at[i, my_c]
        return remote(source, place, att_send.at[i, at_c, t], att_recv.at[i, my_c, t], to)

    def arrived(i, at_c):
        for t in range(tiles + 1):
            place = att_in.at[i, at_c, :, tile(t)] if t < tiles else rest_in.at[i, at_c]
            remote(place, place, att_send.at[i, at_c, t], att_recv.at[i, at_c, t], sib).wait_recv()

    def attend(i, carry):
        at_y = (my_y + i + 1) % rows_y
        bias[...] = jnp.where(doc_col[at_y][:, 0:1] == doc_row, 0.0, -jnp.inf)
        att_acc[...] = jnp.zeros_like(att_acc)
        for h in range(heads):
            lower, upper = head_window(h, group)
            lanes = lax.broadcasted_iota(jnp.int32, (1, upper - lower), 1) + lower
            mine = (lanes >= h * HD) & (lanes < (h + 1) * HD)
            query = qkv[0, at_y, :, :, lower:upper].reshape(CORES * tok, upper - lower)
            query = jnp.where(mine, query.astype(F32), 0.0).astype(BF16)
            keys = qkv[1, :, :, :, lower:upper].reshape(length, upper - lower)
            values = qkv[2, :, :, :, lower:upper].reshape(length, upper - lower)
            scores = lax.dot_general(query, keys, (((1,), (1,)), ((), ())), preferred_element_type=F32)
            scores = scores + bias[...]
            expo = jnp.exp2(scores - jnp.max(scores, axis=1, keepdims=True))
            share = 1.0 / jnp.sum(expo, axis=1, keepdims=True)
            mixed = jnp.dot(expo.astype(BF16), values, preferred_element_type=F32) * share
            att_acc[:, lower:upper] += jnp.where(mine, mixed, 0.0)
            ready = [t for t in range(tiles) if h * HD < (t + 1) * 128 <= (h + 1) * HD]
            for t in ready:
                att_out[i, :, :, tile(t)] = att_acc[:, tile(t)].astype(BF16).reshape(CORES, tok, 128)
            if h == heads - 1:
                spare = att_acc[:, tiles * 128 : group].reshape(CORES, fold, tok // fold, rest)
                spare = jnp.concatenate([spare[:, j] for j in range(fold)], axis=2)
                rest_out[i] = spare.astype(BF16)
                ready = ready + [tiles]

            @pl.when(i < rows_y - 1)
            def _():
                for t in ready:
                    for at_c in range(CORES):
                        attended_copy(i, at_c, t, (me, at_y * CORES + at_c)).start()

        return carry

    lax.fori_loop(0, rows_y, attend, 0)
    last = rows_y - 1
    for t in range(tiles + 1):
        attended_copy(last, 1 - my_c, t, sib).start()
    for c in range(early, len(pieces)):
        forward_weights(c)

    def mixed_out(rows, spare, at_y, at_c):
        spare = spare.astype(F32)
        spare = jnp.concatenate([spare[:, j * rest : (j + 1) * rest] for j in range(fold)], axis=0)
        product = jnp.dot(
            spare.astype(BF16), w_all[at_y, at_c, tiles * 128 : group, :], preferred_element_type=F32
        )
        if tiles:
            product = product + jnp.dot(
                rows[:, : tiles * 128], w_all[at_y, at_c, : tiles * 128, :], preferred_element_type=F32
            )
        return product

    total = mixed_out(att_out[last, my_c], rest_out[last, my_c], my_y, my_c)
    for c in range(len(pieces)):
        weight_copy(c, 0).wait_recv()
        for d in range(1, rows_y):
            weight_forward(c, d, 1 - my_c).wait_recv()
    for i in range(rows_y - 1):
        for at_c in range(CORES):
            arrived(i, at_c)
            total = total + mixed_out(att_in[i, at_c], rest_in[i, at_c], (my_y - i - 1) % rows_y, at_c)
    arrived(last, 1 - my_c)
    total = total + mixed_out(att_in[last, 1 - my_c], rest_in[last, 1 - my_c], my_y, 1 - my_c)
    out[0] = total.astype(BF16)

    for k in range(1, n):
        label_copy(k).wait_send()
    for c in range(len(pieces)):
        for d in range(rows_y):
            token_copy(c, d, my_y).wait_send()
            weight_copy(c, d).wait_send()
            if d:
                token_forward(c, d, my_c).wait_send()
                weight_forward(c, d, my_c).wait_send()
    for i in range(rows_y - 1):
        for at_c in range(CORES):
            for t in range(tiles + 1):
                attended_copy(i, at_c, t, sib).wait_send()
    for t in range(tiles + 1):
        attended_copy(last, 1 - my_c, t, sib).wait_send()


def pass_on(given, out):
    out[...] = given[...]


def body(source, destination, doc_ids, w_qkv, w_out):
    n = lax.axis_size("pack")
    n_seq = lax.axis_size("seq")
    rows_y = n_seq // CORES
    tok, width = source.shape[1:]
    group = w_out.shape[0]
    length = doc_ids.shape[1]
    cap = -(-(2 * tok // n) // 16) * 16
    pieces = [(start, min(256, width - start)) for start in range(0, width, 256)]
    parts = len(pieces)
    rest = group % 128
    fold = 128 // rest
    dma = pltpu.SemaphoreType.DMA
    vmem = pl.BlockSpec(memory_space=pltpu.VMEM)
    result = pl.pallas_call(
        functools.partial(kernel, n, rows_y, cap, pieces),
        out_shape=jax.ShapeDtypeStruct((1, tok, width), BF16),
        in_specs=[vmem] * 3 + [pl.BlockSpec(memory_space=pl.ANY)] * 2,
        out_specs=vmem,
        scratch_shapes=[
            pltpu.VMEM((3, group, width), BF16),
            pltpu.VMEM((n * cap, width), BF16),
            pltpu.VMEM((n * cap, width), BF16),
            pltpu.VMEM((8, n * cap), F32),
            pltpu.VMEM((n, 8, n * cap), F32),
            pltpu.VMEM((rows_y, CORES, tok, width), BF16),
            pltpu.VMEM((3, rows_y, CORES * tok, group), F32),
            pltpu.VMEM((3, rows_y, CORES, tok, group), BF16),
            pltpu.VMEM((rows_y, CORES * tok, 128), F32),
            pltpu.VMEM((CORES * tok, length), F32),
            pltpu.VMEM((CORES * tok, group), F32),
            pltpu.VMEM((rows_y, CORES, tok, group), BF16),
            pltpu.VMEM((rows_y, CORES, tok, group), BF16),
            pltpu.VMEM((rows_y, CORES, tok // fold, rest * fold), BF16),
            pltpu.VMEM((rows_y, CORES, tok // fold, rest * fold), BF16),
            pltpu.VMEM((rows_y, CORES, group, width), BF16),
            dma((parts, n)), dma((parts, n)), dma((n,)), dma((n,)),
            dma((parts, rows_y)), dma((parts, rows_y)), dma((parts, rows_y)), dma((parts, rows_y)),
            dma((parts, rows_y)), dma((parts, rows_y)), dma((parts, rows_y)), dma((parts, rows_y)),
            dma((rows_y, CORES, group // 128 + 1)), dma((rows_y, CORES, group // 128 + 1)), dma((2,)),
        ],
        compiler_params=pltpu.CompilerParams(
            collective_id=0, has_side_effects=True, vmem_limit_bytes=56 * 1024 * 1024
        ),
        cost_estimate=pl.CostEstimate(flops=4_000_000_000, bytes_accessed=4_000_000, transcendentals=2_400_000),
    )(source, destination, doc_ids, jnp.swapaxes(w_qkv, 1, 2), w_out)
    return pl.pallas_call(
        pass_on, out_shape=jax.ShapeDtypeStruct(result.shape, BF16), in_specs=[vmem], out_specs=vmem
    )(result)


def solution(mesh):
    placed = (
        P("seq", "pack", None),
        P("seq", "pack"),
        P("pack", None),
        P(None, None, "seq"),
        P("seq", None),
    )
    return jax.shard_map(
        body, mesh=mesh, in_specs=placed, out_specs=P("pack", "seq", None), check_vma=False
    )
```

```python
import functools
import math

import jax
import jax.numpy as jnp
from jax import lax
from jax.experimental import pallas as pl
from jax.experimental.pallas import tpu as pltpu
from jax.sharding import PartitionSpec as P

HD = 72
CORES = 2
MESH = pl.DeviceIdType.MESH
F32 = jnp.float32
BF16 = jnp.bfloat16


def head_window(head, group):
    lower = head * HD // 128 * 128
    upper = min(-(-(head + 1) * HD // 128) * 128, group)
    return lower, upper


def kernel(
    n, rows_y, cap, pieces,
    src_hbm, dst_hbm, doc_hbm, wqkv_hbm, wout_hbm, out,
    src, dst, doc, wqkv, outbox, inbox, lab_out, lab_in, packed, acc, qkv, doc_col, bias, att_acc, att_out, att_in, rest_out, rest_in, w_all,
    disp_send, disp_recv, lab_send, lab_recv,
    tok_send, tok_recv, tokf_send, tokf_recv,
    w_send, w_recv, wf_send, wf_recv, att_send, att_recv, load_sem,
):
    n_seq = rows_y * CORES
    tok = src.shape[1]
    group = wout_hbm.shape[0]
    length = doc.shape[1]
    heads = group // HD
    me = lax.axis_index("pack")
    seq = lax.axis_index("seq")
    my_y, my_c = seq // CORES, seq % CORES
    sib = (me, my_y * CORES + 1 - my_c)

    half = n // 2
    turns = [*range(half, n), *range(1, half)]

    def peer(k):
        return ((me // half + k // half) % 2 * half + (me % half + k % half) % half, seq)

    def on_y(d):
        return (me, (my_y + d) % rows_y * CORES + my_c)

    def remote(source, target, ss, rs, device):
        return pltpu.make_async_remote_copy(
            src_ref=source, dst_ref=target, send_sem=ss, recv_sem=rs,
            device_id=device, device_id_type=MESH,
        )

    load_qkv = pltpu.make_async_copy(wqkv_hbm, wqkv, load_sem.at[0])
    load_out = pltpu.make_async_copy(wout_hbm, w_all.at[my_y, my_c], load_sem.at[1])
    loads = [
        pltpu.make_async_copy(given, held, load_sem.at[j + 2])
        for j, (given, held) in enumerate([(dst_hbm, dst), (src_hbm, src), (doc_hbm, doc)])
    ]
    for load in loads:
        load.start()
    load_out.start()
    load_qkv.start()

    barrier = pltpu.get_barrier_semaphore()
    for k in range(1, n):
        pl.semaphore_signal(barrier, inc=1, device_id=peer(k), device_id_type=MESH)
    for k in range(1, n_seq):
        pl.semaphore_signal(barrier, inc=1, device_id=(me, (seq + k) % n_seq), device_id_type=MESH)

    for load in loads:
        load.wait()
    dest = dst[...]
    steps = lax.broadcasted_iota(jnp.int32, (n, tok), 0)
    owners = jnp.sum((dest >= (steps + 1) * tok).astype(jnp.int32), axis=0, keepdims=True)
    places = dest - owners * tok
    other = (owners >= half).astype(jnp.int32)
    shift = owners - other * half - me % half
    shift = jnp.where(shift < 0, shift + half, shift)
    shift = shift + jnp.where(other == me // half, 0, half)
    matches = (steps == shift).astype(F32)
    before = lax.broadcasted_iota(jnp.int32, (tok, tok), 0) <= lax.broadcasted_iota(jnp.int32, (tok, tok), 1)
    counted = jnp.dot(matches.astype(BF16), before.astype(F32).astype(BF16), preferred_element_type=F32)
    slots = jnp.sum(matches * counted, axis=0, keepdims=True).astype(jnp.int32) - 1
    flat = shift * cap + slots
    chosen = (lax.broadcasted_iota(jnp.int32, (n * cap, tok), 0) == flat).astype(F32).astype(BF16)
    named = jnp.broadcast_to((places + 1).astype(F32), (8, tok)).astype(BF16)
    lab_out[...] = lax.dot_general(named, chosen, (((1,), (1,)), ((), ())), preferred_element_type=F32)

    def column(c):
        return pl.ds(*pieces[c])

    def fill(c):
        moved = jnp.dot(chosen, src[0, :, column(c)], preferred_element_type=F32).astype(BF16)
        outbox[:, column(c)] = moved
        inbox[0:cap, column(c)] = moved[0:cap]

    def label_copy(k):
        return remote(lab_out, lab_in.at[k], lab_send.at[k], lab_recv.at[k], peer(k))

    def dispatch_copy(c, k):
        block = pl.ds(k * cap, cap)
        return remote(
            outbox.at[block, column(c)], inbox.at[block, column(c)], disp_send.at[c, k], disp_recv.at[c, k],
            peer(k),
        )

    def token_copy(c, d, at_y):
        place = packed.at[at_y, my_c, :, column(c)]
        return remote(place, place, tok_send.at[c, d], tok_recv.at[c, d], on_y(d) if d else sib)

    def token_forward(c, d, at_c):
        place = packed.at[(my_y - d) % rows_y, at_c, :, column(c)]
        return remote(place, place, tokf_send.at[c, d], tokf_recv.at[c, d], sib)

    def weight_copy(c, d):
        place = w_all.at[my_y, my_c, :, column(c)]
        return remote(place, place, w_send.at[c, d], w_recv.at[c, d], on_y(d) if d else sib)

    def weight_forward(c, d, at_c):
        place = w_all.at[(my_y - d) % rows_y, at_c, :, column(c)]
        return remote(place, place, wf_send.at[c, d], wf_recv.at[c, d], sib)

    def send_weights(c):
        for d in range(1, rows_y):
            weight_copy(c, d).start()
        weight_copy(c, 0).start()

    def forward_weights(c):
        for d in range(1, rows_y):
            weight_copy(c, d).wait_recv()
            weight_forward(c, d, my_c).start()

    fill(0)
    pl.semaphore_wait(barrier, n - 1 + n_seq - 1)
    for k in range(1, n):
        label_copy(k).start()
    for c in range(len(pieces)):
        if c:
            fill(c)
        for k in turns:
            dispatch_copy(c, k).start()
        if c == 0:
            load_out.wait()
        if c < len(pieces) - 1:
            send_weights(c)

    doc_row = doc[...].astype(F32)
    doc_col[...] = jnp.broadcast_to(doc_row, (128, length)).T.reshape(doc_col.shape)

    lane = lax.broadcasted_iota(jnp.int32, (1, n * cap), 1)
    label = jnp.where(lane < cap, lab_out[0:1, :], 0.0)
    for k in range(1, n):
        label_copy(k).wait_recv()
        label = jnp.where((lane >= k * cap) & (lane < (k + 1) * cap), lab_in[k, 0:1, :], label)
    rows = lax.broadcasted_iota(jnp.int32, (tok, n * cap), 0) + 1
    placing = (rows.astype(F32) == label).astype(F32).astype(BF16)

    factor = math.log2(math.e) / math.sqrt(HD)

    def project(c, at_y):
        block = packed[at_y, :, :, column(c)].reshape(CORES * tok, pieces[c][1])
        for j in range(3):
            part = lax.dot_general(
                block, wqkv[j, :, column(c)], (((1,), (1,)), ((), ())), preferred_element_type=F32
            )
            if c:
                part = part + acc[j, at_y]
            if c < len(pieces) - 1:
                acc[j, at_y] = part
            else:
                if j == 0:
                    part = part * factor
                qkv[j, at_y] = part.astype(BF16).reshape(CORES, tok, group)

    def consume(c):
        for d in range(1, rows_y):
            token_copy(c, d, (my_y - d) % rows_y).wait_recv()
            token_forward(c, d, my_c).start()
        token_copy(c, 0, my_y).wait_recv()
        project(c, my_y)
        for d in range(1, rows_y):
            token_forward(c, d, 1 - my_c).wait_recv()
            project(c, (my_y - d) % rows_y)

    load_qkv.wait()
    for c in range(len(pieces)):
        for k in range(1, n):
            dispatch_copy(c, k).wait_recv()
        packed[my_y, my_c, :, column(c)] = jnp.dot(
            placing, inbox[:, column(c)], preferred_element_type=F32
        ).astype(BF16)
        for d in range(1, rows_y):
            token_copy(c, d, my_y).start()
        token_copy(c, 0, my_y).start()
        if c:
            consume(c - 1)
            forward_weights(c - 1)
    send_weights(len(pieces) - 1)
    consume(len(pieces) - 1)

    tiles = group // 128
    rest = group - tiles * 128
    fold = tok // rest_out.shape[2]

    def tile(t):
        return pl.ds(t * 128, 128)

    def attended_copy(i, at_c, t, to):
        if t < tiles:
            source, place = att_out.at[i, at_c, :, tile(t)], att_in.at[i, my_c, :, tile(t)]
        else:
            source, place = rest_out.at[i, at_c], rest_in.at[i, my_c]
        return remote(source, place, att_send.at[i, at_c, t], att_recv.at[i, my_c, t], to)

    def arrived(i, at_c):
        for t in range(tiles + 1):
            place = att_in.at[i, at_c, :, tile(t)] if t < tiles else rest_in.at[i, at_c]
            remote(place, place, att_send.at[i, at_c, t], att_recv.at[i, at_c, t], sib).wait_recv()

    def attend(i, carry):
        at_y = (my_y + i + 1) % rows_y
        bias[...] = jnp.where(doc_col[at_y][:, 0:1] == doc_row, 0.0, -jnp.inf)
        att_acc[...] = jnp.zeros_like(att_acc)
        for h in range(heads):
            lower, upper = head_window(h, group)
            lanes = lax.broadcasted_iota(jnp.int32, (1, upper - lower), 1) + lower
            mine = (lanes >= h * HD) & (lanes < (h + 1) * HD)
            query = qkv[0, at_y, :, :, lower:upper].reshape(CORES * tok, upper - lower)
            query = jnp.where(mine, query.astype(F32), 0.0).astype(BF16)
            keys = qkv[1, :, :, :, lower:upper].reshape(length, upper - lower)
            values = qkv[2, :, :, :, lower:upper].reshape(length, upper - lower)
            scores = lax.dot_general(query, keys, (((1,), (1,)), ((), ())), preferred_element_type=F32)
            scores = scores + bias[...]
            expo = jnp.exp2(scores - jnp.max(scores, axis=1, keepdims=True))
            share = 1.0 / jnp.sum(expo, axis=1, keepdims=True)
            mixed = jnp.dot(expo.astype(BF16), values, preferred_element_type=F32) * share
            att_acc[:, lower:upper] += jnp.where(mine, mixed, 0.0)
            ready = [t for t in range(tiles) if h * HD < (t + 1) * 128 <= (h + 1) * HD]
            for t in ready:
                att_out[i, :, :, tile(t)] = att_acc[:, tile(t)].astype(BF16).reshape(CORES, tok, 128)
            if h == heads - 1:
                spare = att_acc[:, tiles * 128 : group].reshape(CORES, fold, tok // fold, rest)
                spare = jnp.concatenate([spare[:, j] for j in range(fold)], axis=2)
                rest_out[i] = spare.astype(BF16)
                ready = ready + [tiles]

            @pl.when(i < rows_y - 1)
            def _():
                for t in ready:
                    for at_c in range(CORES):
                        attended_copy(i, at_c, t, (me, at_y * CORES + at_c)).start()

        return carry

    lax.fori_loop(0, rows_y, attend, 0)
    last = rows_y - 1
    for t in range(tiles + 1):
        attended_copy(last, 1 - my_c, t, sib).start()
    forward_weights(len(pieces) - 1)

    def mixed_out(rows, spare, at_y, at_c):
        spare = spare.astype(F32)
        spare = jnp.concatenate([spare[:, j * rest : (j + 1) * rest] for j in range(fold)], axis=0)
        product = jnp.dot(
            spare.astype(BF16), w_all[at_y, at_c, tiles * 128 : group, :], preferred_element_type=F32
        )
        if tiles:
            product = product + jnp.dot(
                rows[:, : tiles * 128], w_all[at_y, at_c, : tiles * 128, :], preferred_element_type=F32
            )
        return product

    total = mixed_out(att_out[last, my_c], rest_out[last, my_c], my_y, my_c)
    for c in range(len(pieces)):
        weight_copy(c, 0).wait_recv()
        for d in range(1, rows_y):
            weight_forward(c, d, 1 - my_c).wait_recv()
    for i in range(rows_y - 1):
        for at_c in range(CORES):
            arrived(i, at_c)
            total = total + mixed_out(att_in[i, at_c], rest_in[i, at_c], (my_y - i - 1) % rows_y, at_c)
    arrived(last, 1 - my_c)
    total = total + mixed_out(att_in[last, 1 - my_c], rest_in[last, 1 - my_c], my_y, 1 - my_c)
    out[0] = total.astype(BF16)

    for k in range(1, n):
        label_copy(k).wait_send()
    for c in range(len(pieces)):
        for k in range(1, n):
            dispatch_copy(c, k).wait_send()
        for d in range(rows_y):
            token_copy(c, d, my_y).wait_send()
            weight_copy(c, d).wait_send()
            if d:
                token_forward(c, d, my_c).wait_send()
                weight_forward(c, d, my_c).wait_send()
    for i in range(rows_y - 1):
        for at_c in range(CORES):
            for t in range(tiles + 1):
                attended_copy(i, at_c, t, sib).wait_send()
    for t in range(tiles + 1):
        attended_copy(last, 1 - my_c, t, sib).wait_send()


def pass_on(given, out):
    out[...] = given[...]


def body(source, destination, doc_ids, w_qkv, w_out):
    n = lax.axis_size("pack")
    n_seq = lax.axis_size("seq")
    rows_y = n_seq // CORES
    tok, width = source.shape[1:]
    group = w_out.shape[0]
    length = doc_ids.shape[1]
    cap = -(-(2 * tok // n) // 16) * 16
    tiles = width // 128
    ends = [0, tiles - tiles * 5 // 9, tiles - tiles * 2 // 9, tiles]
    pieces = [(start * 128, (end - start) * 128) for start, end in zip(ends, ends[1:])]
    parts = len(pieces)
    rest = group % 128
    fold = 128 // rest
    dma = pltpu.SemaphoreType.DMA
    vmem = pl.BlockSpec(memory_space=pltpu.VMEM)
    result = pl.pallas_call(
        functools.partial(kernel, n, rows_y, cap, pieces),
        out_shape=jax.ShapeDtypeStruct((1, tok, width), BF16),
        in_specs=[pl.BlockSpec(memory_space=pl.ANY)] * 5,
        out_specs=vmem,
        scratch_shapes=[
            pltpu.VMEM(source.shape, BF16),
            pltpu.VMEM(destination.shape, jnp.int32),
            pltpu.VMEM(doc_ids.shape, jnp.int32),
            pltpu.VMEM((3, group, width), BF16),
            pltpu.VMEM((n * cap, width), BF16),
            pltpu.VMEM((n * cap, width), BF16),
            pltpu.VMEM((8, n * cap), F32),
            pltpu.VMEM((n, 8, n * cap), F32),
            pltpu.VMEM((rows_y, CORES, tok, width), BF16),
            pltpu.VMEM((3, rows_y, CORES * tok, group), F32),
            pltpu.VMEM((3, rows_y, CORES, tok, group), BF16),
            pltpu.VMEM((rows_y, CORES * tok, 128), F32),
            pltpu.VMEM((CORES * tok, length), F32),
            pltpu.VMEM((CORES * tok, group), F32),
            pltpu.VMEM((rows_y, CORES, tok, group), BF16),
            pltpu.VMEM((rows_y, CORES, tok, group), BF16),
            pltpu.VMEM((rows_y, CORES, tok // fold, rest * fold), BF16),
            pltpu.VMEM((rows_y, CORES, tok // fold, rest * fold), BF16),
            pltpu.VMEM((rows_y, CORES, group, width), BF16),
            dma((parts, n)), dma((parts, n)), dma((n,)), dma((n,)),
            dma((parts, rows_y)), dma((parts, rows_y)), dma((parts, rows_y)), dma((parts, rows_y)),
            dma((parts, rows_y)), dma((parts, rows_y)), dma((parts, rows_y)), dma((parts, rows_y)),
            dma((rows_y, CORES, group // 128 + 1)), dma((rows_y, CORES, group // 128 + 1)), dma((5,)),
        ],
        compiler_params=pltpu.CompilerParams(
            collective_id=0, has_side_effects=True, vmem_limit_bytes=56 * 1024 * 1024
        ),
        cost_estimate=pl.CostEstimate(flops=4_000_000_000, bytes_accessed=4_000_000, transcendentals=2_400_000),
    )(source, destination, doc_ids, jnp.swapaxes(w_qkv, 1, 2), w_out)
    return pl.pallas_call(
        pass_on, out_shape=jax.ShapeDtypeStruct(result.shape, BF16), in_specs=[vmem], out_specs=vmem
    )(result)


def solution(mesh):
    placed = (
        P("seq", "pack", None),
        P("seq", "pack"),
        P("pack", None),
        P(None, None, "seq"),
        P("seq", None),
    )
    return jax.shard_map(
        body, mesh=mesh, in_specs=placed, out_specs=P("pack", "seq", None), check_vma=False
    )
```

```python
import functools
import math

import jax
import jax.numpy as jnp
from jax import lax
from jax.experimental import pallas as pl
from jax.experimental.pallas import tpu as pltpu
from jax.sharding import PartitionSpec as P

HD = 72
CORES = 2
AHEAD = 2
MESH = pl.DeviceIdType.MESH
F32 = jnp.float32
BF16 = jnp.bfloat16


def head_window(head, group):
    lower = head * HD // 128 * 128
    upper = min(-(-(head + 1) * HD // 128) * 128, group)
    return lower, upper


def kernel(
    n, rows_y, cap, pieces,
    src_hbm, dst_hbm, doc_hbm, wqkv_hbm, wout_hbm, out,
    src, dst, doc, wqkv, outbox, inbox, lab_out, lab_in, packed, acc, qkv, doc_col, bias, att_acc, att_out, att_in, rest_out, rest_in, w_all,
    disp_send, disp_recv, lab_send, lab_recv,
    tok_send, tok_recv, tokf_send, tokf_recv,
    w_send, w_recv, wf_send, wf_recv, att_send, att_recv, load_sem,
):
    n_seq = rows_y * CORES
    tok = src.shape[1]
    group = wout_hbm.shape[0]
    length = doc.shape[1]
    heads = group // HD
    me = lax.axis_index("pack")
    seq = lax.axis_index("seq")
    my_y, my_c = seq // CORES, seq % CORES
    sib = (me, my_y * CORES + 1 - my_c)

    half = n // 2
    turns = [*range(half, n), *range(1, half)]

    def peer(k):
        return ((me // half + k // half) % 2 * half + (me % half + k % half) % half, seq)

    def on_y(d):
        return (me, (my_y + d) % rows_y * CORES + my_c)

    def remote(source, target, ss, rs, device):
        return pltpu.make_async_remote_copy(
            src_ref=source, dst_ref=target, send_sem=ss, recv_sem=rs,
            device_id=device, device_id_type=MESH,
        )

    load_qkv = pltpu.make_async_copy(wqkv_hbm, wqkv, load_sem.at[0])
    load_out = pltpu.make_async_copy(wout_hbm, w_all.at[my_y, my_c], load_sem.at[1])
    loads = [
        pltpu.make_async_copy(given, held, load_sem.at[j + 2])
        for j, (given, held) in enumerate([(dst_hbm, dst), (src_hbm, src), (doc_hbm, doc)])
    ]
    for load in loads:
        load.start()
    load_out.start()
    load_qkv.start()

    barrier = pltpu.get_barrier_semaphore()
    for k in range(1, n):
        pl.semaphore_signal(barrier, inc=1, device_id=peer(k), device_id_type=MESH)
    for k in range(1, n_seq):
        pl.semaphore_signal(barrier, inc=1, device_id=(me, (seq + k) % n_seq), device_id_type=MESH)

    for load in loads:
        load.wait()
    dest = dst[...]
    steps = lax.broadcasted_iota(jnp.int32, (n, tok), 0)
    owners = jnp.sum((dest >= (steps + 1) * tok).astype(jnp.int32), axis=0, keepdims=True)
    places = dest - owners * tok
    other = (owners >= half).astype(jnp.int32)
    shift = owners - other * half - me % half
    shift = jnp.where(shift < 0, shift + half, shift)
    shift = shift + jnp.where(other == me // half, 0, half)
    matches = (steps == shift).astype(F32)
    before = lax.broadcasted_iota(jnp.int32, (tok, tok), 0) <= lax.broadcasted_iota(jnp.int32, (tok, tok), 1)
    counted = jnp.dot(matches.astype(BF16), before.astype(F32).astype(BF16), preferred_element_type=F32)
    slots = jnp.sum(matches * counted, axis=0, keepdims=True).astype(jnp.int32) - 1
    flat = shift * cap + slots
    chosen = (lax.broadcasted_iota(jnp.int32, (n * cap, tok), 0) == flat).astype(F32).astype(BF16)
    named = jnp.broadcast_to((places + 1).astype(F32), (8, tok)).astype(BF16)
    lab_out[...] = lax.dot_general(named, chosen, (((1,), (1,)), ((), ())), preferred_element_type=F32)

    def column(c):
        return pl.ds(*pieces[c])

    def fill(c):
        moved = jnp.dot(chosen, src[0, :, column(c)], preferred_element_type=F32).astype(BF16)
        outbox[:, column(c)] = moved
        inbox[0:cap, column(c)] = moved[0:cap]

    def label_copy(k):
        return remote(lab_out, lab_in.at[k], lab_send.at[k], lab_recv.at[k], peer(k))

    def dispatch_copy(c, k):
        block = pl.ds(k * cap, cap)
        return remote(
            outbox.at[block, column(c)], inbox.at[block, column(c)], disp_send.at[c, k], disp_recv.at[c, k],
            peer(k),
        )

    def token_copy(c, d, at_y):
        place = packed.at[at_y, my_c, :, column(c)]
        return remote(place, place, tok_send.at[c, d], tok_recv.at[c, d], on_y(d) if d else sib)

    def token_forward(c, d, at_c):
        place = packed.at[(my_y - d) % rows_y, at_c, :, column(c)]
        return remote(place, place, tokf_send.at[c, d], tokf_recv.at[c, d], sib)

    def weight_copy(c, d):
        place = w_all.at[my_y, my_c, :, column(c)]
        return remote(place, place, w_send.at[c, d], w_recv.at[c, d], on_y(d) if d else sib)

    def weight_forward(c, d, at_c):
        place = w_all.at[(my_y - d) % rows_y, at_c, :, column(c)]
        return remote(place, place, wf_send.at[c, d], wf_recv.at[c, d], sib)

    def send_weights(c):
        for d in range(1, rows_y):
            weight_copy(c, d).start()
        weight_copy(c, 0).start()

    def forward_weights(c):
        for d in range(1, rows_y):
            weight_copy(c, d).wait_recv()
            weight_forward(c, d, my_c).start()

    fill(0)
    pl.semaphore_wait(barrier, n - 1 + n_seq - 1)
    for k in range(1, n):
        label_copy(k).start()
    for c in range(len(pieces)):
        if c:
            fill(c)
        if c < AHEAD:
            for k in turns:
                dispatch_copy(c, k).start()
        if c == 0:
            load_out.wait()
        if c < len(pieces) - 1:
            send_weights(c)

    doc_row = doc[...].astype(F32)
    doc_col[...] = jnp.broadcast_to(doc_row, (128, length)).T.reshape(doc_col.shape)

    lane = lax.broadcasted_iota(jnp.int32, (1, n * cap), 1)
    label = jnp.where(lane < cap, lab_out[0:1, :], 0.0)
    for k in range(1, n):
        label_copy(k).wait_recv()
        label = jnp.where((lane >= k * cap) & (lane < (k + 1) * cap), lab_in[k, 0:1, :], label)
    rows = lax.broadcasted_iota(jnp.int32, (tok, n * cap), 0) + 1
    placing = (rows.astype(F32) == label).astype(F32).astype(BF16)

    factor = math.log2(math.e) / math.sqrt(HD)

    def project(c, at_y):
        block = packed[at_y, :, :, column(c)].reshape(CORES * tok, pieces[c][1])
        for j in range(3):
            part = lax.dot_general(
                block, wqkv[j, :, column(c)], (((1,), (1,)), ((), ())), preferred_element_type=F32
            )
            if c:
                part = part + acc[j, at_y]
            if c < len(pieces) - 1:
                acc[j, at_y] = part
            else:
                if j == 0:
                    part = part * factor
                qkv[j, at_y] = part.astype(BF16).reshape(CORES, tok, group)

    def consume(c):
        for d in range(1, rows_y):
            token_copy(c, d, (my_y - d) % rows_y).wait_recv()
            token_forward(c, d, my_c).start()
        token_copy(c, 0, my_y).wait_recv()
        project(c, my_y)
        for d in range(1, rows_y):
            token_forward(c, d, 1 - my_c).wait_recv()
            project(c, (my_y - d) % rows_y)

    load_qkv.wait()
    for c in range(len(pieces)):
        for k in turns:
            dispatch_copy(c, k).wait_send()
            if c + AHEAD < len(pieces):
                dispatch_copy(c + AHEAD, k).start()
        for k in range(1, n):
            dispatch_copy(c, k).wait_recv()
        packed[my_y, my_c, :, column(c)] = jnp.dot(
            placing, inbox[:, column(c)], preferred_element_type=F32
        ).astype(BF16)
        for d in range(1, rows_y):
            token_copy(c, d, my_y).start()
        token_copy(c, 0, my_y).start()
        if c:
            consume(c - 1)
            forward_weights(c - 1)
    send_weights(len(pieces) - 1)
    consume(len(pieces) - 1)

    tiles = group // 128
    rest = group - tiles * 128
    fold = tok // rest_out.shape[2]

    def tile(t):
        return pl.ds(t * 128, 128)

    def attended_copy(i, at_c, t, to):
        if t < tiles:
            source, place = att_out.at[i, at_c, :, tile(t)], att_in.at[i, my_c, :, tile(t)]
        else:
            source, place = rest_out.at[i, at_c], rest_in.at[i, my_c]
        return remote(source, place, att_send.at[i, at_c, t], att_recv.at[i, my_c, t], to)

    def arrived(i, at_c):
        for t in range(tiles + 1):
            place = att_in.at[i, at_c, :, tile(t)] if t < tiles else rest_in.at[i, at_c]
            remote(place, place, att_send.at[i, at_c, t], att_recv.at[i, at_c, t], sib).wait_recv()

    def attend(i, carry):
        at_y = (my_y + i + 1) % rows_y
        bias[...] = jnp.where(doc_col[at_y][:, 0:1] == doc_row, 0.0, -jnp.inf)
        att_acc[...] = jnp.zeros_like(att_acc)
        for h in range(heads):
            lower, upper = head_window(h, group)
            lanes = lax.broadcasted_iota(jnp.int32, (1, upper - lower), 1) + lower
            mine = (lanes >= h * HD) & (lanes < (h + 1) * HD)
            query = qkv[0, at_y, :, :, lower:upper].reshape(CORES * tok, upper - lower)
            query = jnp.where(mine, query.astype(F32), 0.0).astype(BF16)
            keys = qkv[1, :, :, :, lower:upper].reshape(length, upper - lower)
            values = qkv[2, :, :, :, lower:upper].reshape(length, upper - lower)
            scores = lax.dot_general(query, keys, (((1,), (1,)), ((), ())), preferred_element_type=F32)
            scores = scores + bias[...]
            expo = jnp.exp2(scores - jnp.max(scores, axis=1, keepdims=True))
            share = 1.0 / jnp.sum(expo, axis=1, keepdims=True)
            mixed = jnp.dot(expo.astype(BF16), values, preferred_element_type=F32) * share
            att_acc[:, lower:upper] += jnp.where(mine, mixed, 0.0)
            ready = [t for t in range(tiles) if h * HD < (t + 1) * 128 <= (h + 1) * HD]
            for t in ready:
                att_out[i, :, :, tile(t)] = att_acc[:, tile(t)].astype(BF16).reshape(CORES, tok, 128)
            if h == heads - 1:
                spare = att_acc[:, tiles * 128 : group].reshape(CORES, fold, tok // fold, rest)
                spare = jnp.concatenate([spare[:, j] for j in range(fold)], axis=2)
                rest_out[i] = spare.astype(BF16)
                ready = ready + [tiles]

            @pl.when(i < rows_y - 1)
            def _():
                for t in ready:
                    for at_c in range(CORES):
                        attended_copy(i, at_c, t, (me, at_y * CORES + at_c)).start()

        return carry

    lax.fori_loop(0, rows_y, attend, 0)
    last = rows_y - 1
    for t in range(tiles + 1):
        attended_copy(last, 1 - my_c, t, sib).start()
    forward_weights(len(pieces) - 1)

    def mixed_out(rows, spare, at_y, at_c):
        spare = spare.astype(F32)
        spare = jnp.concatenate([spare[:, j * rest : (j + 1) * rest] for j in range(fold)], axis=0)
        product = jnp.dot(
            spare.astype(BF16), w_all[at_y, at_c, tiles * 128 : group, :], preferred_element_type=F32
        )
        if tiles:
            product = product + jnp.dot(
                rows[:, : tiles * 128], w_all[at_y, at_c, : tiles * 128, :], preferred_element_type=F32
            )
        return product

    total = mixed_out(att_out[last, my_c], rest_out[last, my_c], my_y, my_c)
    for c in range(len(pieces)):
        weight_copy(c, 0).wait_recv()
        for d in range(1, rows_y):
            weight_forward(c, d, 1 - my_c).wait_recv()
    for i in range(rows_y - 1):
        for at_c in range(CORES):
            arrived(i, at_c)
            total = total + mixed_out(att_in[i, at_c], rest_in[i, at_c], (my_y - i - 1) % rows_y, at_c)
    arrived(last, 1 - my_c)
    total = total + mixed_out(att_in[last, 1 - my_c], rest_in[last, 1 - my_c], my_y, 1 - my_c)
    out[0] = total.astype(BF16)

    for k in range(1, n):
        label_copy(k).wait_send()
    for c in range(len(pieces)):
        for d in range(rows_y):
            token_copy(c, d, my_y).wait_send()
            weight_copy(c, d).wait_send()
            if d:
                token_forward(c, d, my_c).wait_send()
                weight_forward(c, d, my_c).wait_send()
    for i in range(rows_y - 1):
        for at_c in range(CORES):
            for t in range(tiles + 1):
                attended_copy(i, at_c, t, sib).wait_send()
    for t in range(tiles + 1):
        attended_copy(last, 1 - my_c, t, sib).wait_send()


def pass_on(given, out):
    out[...] = given[...]


def body(source, destination, doc_ids, w_qkv, w_out):
    n = lax.axis_size("pack")
    n_seq = lax.axis_size("seq")
    rows_y = n_seq // CORES
    tok, width = source.shape[1:]
    group = w_out.shape[0]
    length = doc_ids.shape[1]
    cap = -(-(2 * tok // n) // 16) * 16
    tiles = width // 128
    ends = [0, tiles - tiles * 5 // 9, tiles - tiles * 2 // 9, tiles]
    pieces = [(start * 128, (end - start) * 128) for start, end in zip(ends, ends[1:])]
    parts = len(pieces)
    rest = group % 128
    fold = 128 // rest
    dma = pltpu.SemaphoreType.DMA
    vmem = pl.BlockSpec(memory_space=pltpu.VMEM)
    result = pl.pallas_call(
        functools.partial(kernel, n, rows_y, cap, pieces),
        out_shape=jax.ShapeDtypeStruct((1, tok, width), BF16),
        in_specs=[pl.BlockSpec(memory_space=pl.ANY)] * 5,
        out_specs=vmem,
        scratch_shapes=[
            pltpu.VMEM(source.shape, BF16),
            pltpu.VMEM(destination.shape, jnp.int32),
            pltpu.VMEM(doc_ids.shape, jnp.int32),
            pltpu.VMEM((3, group, width), BF16),
            pltpu.VMEM((n * cap, width), BF16),
            pltpu.VMEM((n * cap, width), BF16),
            pltpu.VMEM((8, n * cap), F32),
            pltpu.VMEM((n, 8, n * cap), F32),
            pltpu.VMEM((rows_y, CORES, tok, width), BF16),
            pltpu.VMEM((3, rows_y, CORES * tok, group), F32),
            pltpu.VMEM((3, rows_y, CORES, tok, group), BF16),
            pltpu.VMEM((rows_y, CORES * tok, 128), F32),
            pltpu.VMEM((CORES * tok, length), F32),
            pltpu.VMEM((CORES * tok, group), F32),
            pltpu.VMEM((rows_y, CORES, tok, group), BF16),
            pltpu.VMEM((rows_y, CORES, tok, group), BF16),
            pltpu.VMEM((rows_y, CORES, tok // fold, rest * fold), BF16),
            pltpu.VMEM((rows_y, CORES, tok // fold, rest * fold), BF16),
            pltpu.VMEM((rows_y, CORES, group, width), BF16),
            dma((parts, n)), dma((parts, n)), dma((n,)), dma((n,)),
            dma((parts, rows_y)), dma((parts, rows_y)), dma((parts, rows_y)), dma((parts, rows_y)),
            dma((parts, rows_y)), dma((parts, rows_y)), dma((parts, rows_y)), dma((parts, rows_y)),
            dma((rows_y, CORES, group // 128 + 1)), dma((rows_y, CORES, group // 128 + 1)), dma((5,)),
        ],
        compiler_params=pltpu.CompilerParams(
            collective_id=0, has_side_effects=True, vmem_limit_bytes=56 * 1024 * 1024
        ),
        cost_estimate=pl.CostEstimate(flops=4_000_000_000, bytes_accessed=4_000_000, transcendentals=2_400_000),
    )(source, destination, doc_ids, jnp.swapaxes(w_qkv, 1, 2), w_out)
    return pl.pallas_call(
        pass_on, out_shape=jax.ShapeDtypeStruct(result.shape, BF16), in_specs=[vmem], out_specs=vmem
    )(result)


def solution(mesh):
    placed = (
        P("seq", "pack", None),
        P("seq", "pack"),
        P("pack", None),
        P(None, None, "seq"),
        P("seq", None),
    )
    return jax.shard_map(
        body, mesh=mesh, in_specs=placed, out_specs=P("pack", "seq", None), check_vma=False
    )
```

```python
import functools
import math

import jax
import jax.numpy as jnp
from jax import lax
from jax.experimental import pallas as pl
from jax.experimental.pallas import tpu as pltpu
from jax.sharding import PartitionSpec as P

HD = 72
CORES = 2
AHEAD = 2
MESH = pl.DeviceIdType.MESH
F32 = jnp.float32
BF16 = jnp.bfloat16


def head_window(head, group):
    lower = head * HD // 128 * 128
    upper = min(-(-(head + 1) * HD // 128) * 128, group)
    return lower, upper


def kernel(
    n, rows_y, cap, pieces,
    src_hbm, dst_hbm, doc_hbm, wqkv_hbm, wout_hbm, out,
    src, dst, doc, wqkv, outbox, inbox, lab_out, lab_in, packed, acc, qkv, doc_col, bias, att_acc, att_out, att_in, rest_out, rest_in, w_all,
    disp_send, disp_recv, lab_send, lab_recv,
    tok_send, tok_recv, tokf_send, tokf_recv,
    w_send, w_recv, wf_send, wf_recv, att_send, att_recv, load_sem,
):
    n_seq = rows_y * CORES
    early = len(pieces) * 3 // 5
    tok = src.shape[1]
    group = wout_hbm.shape[0]
    length = doc.shape[1]
    heads = group // HD
    me = lax.axis_index("pack")
    seq = lax.axis_index("seq")
    my_y, my_c = seq // CORES, seq % CORES
    sib = (me, my_y * CORES + 1 - my_c)

    half = n // 2
    turns = [*range(half, n), *range(1, half)]

    def peer(k):
        return ((me // half + k // half) % 2 * half + (me % half + k % half) % half, seq)

    def on_y(d):
        return (me, (my_y + d) % rows_y * CORES + my_c)

    def remote(source, target, ss, rs, device):
        return pltpu.make_async_remote_copy(
            src_ref=source, dst_ref=target, send_sem=ss, recv_sem=rs,
            device_id=device, device_id_type=MESH,
        )

    load_qkv = pltpu.make_async_copy(wqkv_hbm, wqkv, load_sem.at[0])
    load_out = pltpu.make_async_copy(wout_hbm, w_all.at[my_y, my_c], load_sem.at[1])
    loads = [
        pltpu.make_async_copy(given, held, load_sem.at[j + 2])
        for j, (given, held) in enumerate([(dst_hbm, dst), (src_hbm, src), (doc_hbm, doc)])
    ]
    for load in loads:
        load.start()
    load_out.start()
    load_qkv.start()

    barrier = pltpu.get_barrier_semaphore()
    for k in range(1, n):
        pl.semaphore_signal(barrier, inc=1, device_id=peer(k), device_id_type=MESH)
    for k in range(1, n_seq):
        pl.semaphore_signal(barrier, inc=1, device_id=(me, (seq + k) % n_seq), device_id_type=MESH)

    for load in loads:
        load.wait()
    dest = dst[...]
    steps = lax.broadcasted_iota(jnp.int32, (n, tok), 0)
    owners = jnp.sum((dest >= (steps + 1) * tok).astype(jnp.int32), axis=0, keepdims=True)
    places = dest - owners * tok
    other = (owners >= half).astype(jnp.int32)
    shift = owners - other * half - me % half
    shift = jnp.where(shift < 0, shift + half, shift)
    shift = shift + jnp.where(other == me // half, 0, half)
    matches = (steps == shift).astype(F32)
    before = lax.broadcasted_iota(jnp.int32, (tok, tok), 0) <= lax.broadcasted_iota(jnp.int32, (tok, tok), 1)
    counted = jnp.dot(matches.astype(BF16), before.astype(F32).astype(BF16), preferred_element_type=F32)
    slots = jnp.sum(matches * counted, axis=0, keepdims=True).astype(jnp.int32) - 1
    flat = shift * cap + slots
    chosen = (lax.broadcasted_iota(jnp.int32, (n * cap, tok), 0) == flat).astype(F32).astype(BF16)
    named = jnp.broadcast_to((places + 1).astype(F32), (8, tok)).astype(BF16)
    lab_out[...] = lax.dot_general(named, chosen, (((1,), (1,)), ((), ())), preferred_element_type=F32)

    def column(c):
        return pl.ds(*pieces[c])

    def fill(c):
        moved = jnp.dot(chosen, src[0, :, column(c)], preferred_element_type=F32).astype(BF16)
        outbox[:, column(c)] = moved
        inbox[0:cap, column(c)] = moved[0:cap]

    def label_copy(k):
        return remote(lab_out, lab_in.at[k], lab_send.at[k], lab_recv.at[k], peer(k))

    def dispatch_copy(c, k):
        block = pl.ds(k * cap, cap)
        return remote(
            outbox.at[block, column(c)], inbox.at[block, column(c)], disp_send.at[c, k], disp_recv.at[c, k],
            peer(k),
        )

    def token_copy(c, d, at_y):
        place = packed.at[at_y, my_c, :, column(c)]
        return remote(place, place, tok_send.at[c, d], tok_recv.at[c, d], on_y(d) if d else sib)

    def token_forward(c, d, at_c):
        place = packed.at[(my_y - d) % rows_y, at_c, :, column(c)]
        return remote(place, place, tokf_send.at[c, d], tokf_recv.at[c, d], sib)

    def weight_copy(c, d):
        place = w_all.at[my_y, my_c, :, column(c)]
        return remote(place, place, w_send.at[c, d], w_recv.at[c, d], on_y(d) if d else sib)

    def weight_forward(c, d, at_c):
        place = w_all.at[(my_y - d) % rows_y, at_c, :, column(c)]
        return remote(place, place, wf_send.at[c, d], wf_recv.at[c, d], sib)

    def send_weights(c):
        for d in range(1, rows_y):
            weight_copy(c, d).start()
        weight_copy(c, 0).start()

    def forward_weights(c):
        for d in range(1, rows_y):
            weight_copy(c, d).wait_recv()
            weight_forward(c, d, my_c).start()

    fill(0)
    pl.semaphore_wait(barrier, n - 1 + n_seq - 1)
    for k in range(1, n):
        label_copy(k).start()
    for c in range(len(pieces)):
        if c:
            fill(c)
        if c < AHEAD:
            for k in turns:
                dispatch_copy(c, k).start()
        if c == 0:
            load_out.wait()
        if c < early:
            send_weights(c)

    doc_row = doc[...].astype(F32)
    doc_col[...] = jnp.broadcast_to(doc_row, (128, length)).T.reshape(doc_col.shape)

    lane = lax.broadcasted_iota(jnp.int32, (1, n * cap), 1)
    label = jnp.where(lane < cap, lab_out[0:1, :], 0.0)
    for k in range(1, n):
        label_copy(k).wait_recv()
        label = jnp.where((lane >= k * cap) & (lane < (k + 1) * cap), lab_in[k, 0:1, :], label)
    rows = lax.broadcasted_iota(jnp.int32, (tok, n * cap), 0) + 1
    placing = (rows.astype(F32) == label).astype(F32).astype(BF16)

    factor = math.log2(math.e) / math.sqrt(HD)

    def project(c, at_y):
        block = packed[at_y, :, :, column(c)].reshape(CORES * tok, pieces[c][1])
        for j in range(3):
            part = lax.dot_general(
                block, wqkv[j, :, column(c)], (((1,), (1,)), ((), ())), preferred_element_type=F32
            )
            if c:
                part = part + acc[j, at_y]
            if c < len(pieces) - 1:
                acc[j, at_y] = part
            else:
                if j == 0:
                    part = part * factor
                qkv[j, at_y] = part.astype(BF16).reshape(CORES, tok, group)

    def consume(c):
        for d in range(1, rows_y):
            token_copy(c, d, (my_y - d) % rows_y).wait_recv()
            token_forward(c, d, my_c).start()
        token_copy(c, 0, my_y).wait_recv()
        project(c, my_y)
        for d in range(1, rows_y):
            token_forward(c, d, 1 - my_c).wait_recv()
            project(c, (my_y - d) % rows_y)

    load_qkv.wait()
    for c in range(len(pieces)):
        for k in turns:
            dispatch_copy(c, k).wait_send()
            if c + AHEAD < len(pieces):
                dispatch_copy(c + AHEAD, k).start()
        for k in range(1, n):
            dispatch_copy(c, k).wait_recv()
        packed[my_y, my_c, :, column(c)] = jnp.dot(
            placing, inbox[:, column(c)], preferred_element_type=F32
        ).astype(BF16)
        for d in range(1, rows_y):
            token_copy(c, d, my_y).start()
        token_copy(c, 0, my_y).start()
        if c:
            consume(c - 1)
            if c - 1 < early:
                forward_weights(c - 1)
    for c in range(early, len(pieces)):
        send_weights(c)
    consume(len(pieces) - 1)

    tiles = group // 128
    rest = group - tiles * 128
    fold = tok // rest_out.shape[2]

    def tile(t):
        return pl.ds(t * 128, 128)

    def attended_copy(i, at_c, t, to):
        if t < tiles:
            source, place = att_out.at[i, at_c, :, tile(t)], att_in.at[i, my_c, :, tile(t)]
        else:
            source, place = rest_out.at[i, at_c], rest_in.at[i, my_c]
        return remote(source, place, att_send.at[i, at_c, t], att_recv.at[i, my_c, t], to)

    def arrived(i, at_c):
        for t in range(tiles + 1):
            place = att_in.at[i, at_c, :, tile(t)] if t < tiles else rest_in.at[i, at_c]
            remote(place, place, att_send.at[i, at_c, t], att_recv.at[i, at_c, t], sib).wait_recv()

    def attend(i, carry):
        at_y = (my_y + i + 1) % rows_y
        bias[...] = jnp.where(doc_col[at_y][:, 0:1] == doc_row, 0.0, -jnp.inf)
        att_acc[...] = jnp.zeros_like(att_acc)
        for h in range(heads):
            lower, upper = head_window(h, group)
            lanes = lax.broadcasted_iota(jnp.int32, (1, upper - lower), 1) + lower
            mine = (lanes >= h * HD) & (lanes < (h + 1) * HD)
            query = qkv[0, at_y, :, :, lower:upper].reshape(CORES * tok, upper - lower)
            query = jnp.where(mine, query.astype(F32), 0.0).astype(BF16)
            keys = qkv[1, :, :, :, lower:upper].reshape(length, upper - lower)
            values = qkv[2, :, :, :, lower:upper].reshape(length, upper - lower)
            scores = lax.dot_general(query, keys, (((1,), (1,)), ((), ())), preferred_element_type=F32)
            scores = scores + bias[...]
            expo = jnp.exp2(scores - jnp.max(scores, axis=1, keepdims=True))
            share = 1.0 / jnp.sum(expo, axis=1, keepdims=True)
            mixed = jnp.dot(expo.astype(BF16), values, preferred_element_type=F32) * share
            att_acc[:, lower:upper] += jnp.where(mine, mixed, 0.0)
            ready = [t for t in range(tiles) if h * HD < (t + 1) * 128 <= (h + 1) * HD]
            for t in ready:
                att_out[i, :, :, tile(t)] = att_acc[:, tile(t)].astype(BF16).reshape(CORES, tok, 128)
            if h == heads - 1:
                spare = att_acc[:, tiles * 128 : group].reshape(CORES, fold, tok // fold, rest)
                spare = jnp.concatenate([spare[:, j] for j in range(fold)], axis=2)
                rest_out[i] = spare.astype(BF16)
                ready = ready + [tiles]

            @pl.when(i < rows_y - 1)
            def _():
                for t in ready:
                    for at_c in range(CORES):
                        attended_copy(i, at_c, t, (me, at_y * CORES + at_c)).start()

        return carry

    lax.fori_loop(0, rows_y, attend, 0)
    last = rows_y - 1
    for t in range(tiles + 1):
        attended_copy(last, 1 - my_c, t, sib).start()
    for c in range(early, len(pieces)):
        forward_weights(c)

    def mixed_out(rows, spare, at_y, at_c):
        spare = spare.astype(F32)
        spare = jnp.concatenate([spare[:, j * rest : (j + 1) * rest] for j in range(fold)], axis=0)
        product = jnp.dot(
            spare.astype(BF16), w_all[at_y, at_c, tiles * 128 : group, :], preferred_element_type=F32
        )
        if tiles:
            product = product + jnp.dot(
                rows[:, : tiles * 128], w_all[at_y, at_c, : tiles * 128, :], preferred_element_type=F32
            )
        return product

    total = mixed_out(att_out[last, my_c], rest_out[last, my_c], my_y, my_c)
    for c in range(len(pieces)):
        weight_copy(c, 0).wait_recv()
        for d in range(1, rows_y):
            weight_forward(c, d, 1 - my_c).wait_recv()
    for i in range(rows_y - 1):
        for at_c in range(CORES):
            arrived(i, at_c)
            total = total + mixed_out(att_in[i, at_c], rest_in[i, at_c], (my_y - i - 1) % rows_y, at_c)
    arrived(last, 1 - my_c)
    total = total + mixed_out(att_in[last, 1 - my_c], rest_in[last, 1 - my_c], my_y, 1 - my_c)
    out[0] = total.astype(BF16)

    for k in range(1, n):
        label_copy(k).wait_send()
    for c in range(len(pieces)):
        for d in range(rows_y):
            token_copy(c, d, my_y).wait_send()
            weight_copy(c, d).wait_send()
            if d:
                token_forward(c, d, my_c).wait_send()
                weight_forward(c, d, my_c).wait_send()
    for i in range(rows_y - 1):
        for at_c in range(CORES):
            for t in range(tiles + 1):
                attended_copy(i, at_c, t, sib).wait_send()
    for t in range(tiles + 1):
        attended_copy(last, 1 - my_c, t, sib).wait_send()


def pass_on(given, out):
    out[...] = given[...]


def body(source, destination, doc_ids, w_qkv, w_out):
    n = lax.axis_size("pack")
    n_seq = lax.axis_size("seq")
    rows_y = n_seq // CORES
    tok, width = source.shape[1:]
    group = w_out.shape[0]
    length = doc_ids.shape[1]
    cap = -(-(2 * tok // n) // 16) * 16
    pieces = [(start, min(256, width - start)) for start in range(0, width, 256)]
    parts = len(pieces)
    rest = group % 128
    fold = 128 // rest
    dma = pltpu.SemaphoreType.DMA
    vmem = pl.BlockSpec(memory_space=pltpu.VMEM)
    result = pl.pallas_call(
        functools.partial(kernel, n, rows_y, cap, pieces),
        out_shape=jax.ShapeDtypeStruct((1, tok, width), BF16),
        in_specs=[pl.BlockSpec(memory_space=pl.ANY)] * 5,
        out_specs=vmem,
        scratch_shapes=[
            pltpu.VMEM(source.shape, BF16),
            pltpu.VMEM(destination.shape, jnp.int32),
            pltpu.VMEM(doc_ids.shape, jnp.int32),
            pltpu.VMEM((3, group, width), BF16),
            pltpu.VMEM((n * cap, width), BF16),
            pltpu.VMEM((n * cap, width), BF16),
            pltpu.VMEM((8, n * cap), F32),
            pltpu.VMEM((n, 8, n * cap), F32),
            pltpu.VMEM((rows_y, CORES, tok, width), BF16),
            pltpu.VMEM((3, rows_y, CORES * tok, group), F32),
            pltpu.VMEM((3, rows_y, CORES, tok, group), BF16),
            pltpu.VMEM((rows_y, CORES * tok, 128), F32),
            pltpu.VMEM((CORES * tok, length), F32),
            pltpu.VMEM((CORES * tok, group), F32),
            pltpu.VMEM((rows_y, CORES, tok, group), BF16),
            pltpu.VMEM((rows_y, CORES, tok, group), BF16),
            pltpu.VMEM((rows_y, CORES, tok // fold, rest * fold), BF16),
            pltpu.VMEM((rows_y, CORES, tok // fold, rest * fold), BF16),
            pltpu.VMEM((rows_y, CORES, group, width), BF16),
            dma((parts, n)), dma((parts, n)), dma((n,)), dma((n,)),
            dma((parts, rows_y)), dma((parts, rows_y)), dma((parts, rows_y)), dma((parts, rows_y)),
            dma((parts, rows_y)), dma((parts, rows_y)), dma((parts, rows_y)), dma((parts, rows_y)),
            dma((rows_y, CORES, group // 128 + 1)), dma((rows_y, CORES, group // 128 + 1)), dma((5,)),
        ],
        compiler_params=pltpu.CompilerParams(
            collective_id=0, has_side_effects=True, vmem_limit_bytes=56 * 1024 * 1024
        ),
        cost_estimate=pl.CostEstimate(flops=4_000_000_000, bytes_accessed=4_000_000, transcendentals=2_400_000),
    )(source, destination, doc_ids, jnp.swapaxes(w_qkv, 1, 2), w_out)
    return pl.pallas_call(
        pass_on, out_shape=jax.ShapeDtypeStruct(result.shape, BF16), in_specs=[vmem], out_specs=vmem
    )(result)


def solution(mesh):
    placed = (
        P("seq", "pack", None),
        P("seq", "pack"),
        P("pack", None),
        P(None, None, "seq"),
        P("seq", None),
    )
    return jax.shard_map(
        body, mesh=mesh, in_specs=placed, out_specs=P("pack", "seq", None), check_vma=False
    )
```
